256 devices in a mesh: dp: 4 (over x_lo, core), cent: 64 (over z, y, x_hi).
Axes of the slice: x: 4 (x_hi: 2, x_lo: 2; x = x_hi * 2 + x_lo), y: 4, z: 8, core: 2. Of those that a mesh axis runs over, the one named last changes fastest.
Arguments:
- embeddings: bfloat16 [8192, 768], P('dp'), may hold values from -40 to 40
- centroids: float32 [65536, 768], P('cent'), may hold values from -0.5 to 0.5
Outputs:
- new_centroids: float32 [65536, 768], P('cent')
- log_total: float32 [8192], P('dp')
The draws below stay inside these ranges and needn't reach their ends.
All inputs are finite; a program needn't handle non-finite values.
Results may differ from the reference program's by a relative error of at most 0.012.
The reference program's roundings to bfloat16 on the way (of `rounded` and `weights`) count: a program that leaves them out, or rounds other values in their place, can miss the bound.
Values sent between devices are 32-bit elements; how exact they have to be, the bound alone decides.
A program may use at most 64 MiB of HBM per device.

```python
import jax
import jax.numpy as jnp
from jax import lax

D = 768
KDEV = 1024
R_DEV = 2048
ITERS = 2
K = 65536
ROWS = 8192
N_CENT = 64


logit_divisor = 0.05


def shared_centroids(key, upper):
    key = jax.random.fold_in(key, 101)
    first, second = jax.random.split(key)
    scales = jnp.exp(jax.random.uniform(first, (K, 1), jnp.float32, jnp.log(0.5), jnp.log(upper)))
    base = jax.random.truncated_normal(second, -4.0, 4.0, (K, D), jnp.float32)
    return jnp.clip(base * scales * D ** (-0.5), -0.49, 0.49)


def captured_rows(key, centers, low, high):
    shard_count = ROWS // R_DEV
    first, second, third = jax.random.split(key, 3)
    positions = jnp.arange(ROWS)
    shard = positions // R_DEV
    local = positions % R_DEV
    block_ids = jax.random.randint(first, (shard_count,), 0, K // KDEV)
    orders = jax.vmap(lambda item: jax.random.permutation(item, KDEV))(jax.random.split(second, shard_count))
    chosen = block_ids[shard] * KDEV + orders[shard, local % KDEV]
    heads = centers[chosen]
    pull = jax.random.uniform(third, (ROWS,), jnp.float32, low, high)
    length_energy = jnp.sum(heads * heads, axis=1)
    ratio = 0.5 + logit_divisor * pull / length_energy
    return (ratio[:, None] * heads, local < R_DEV // 2)


def draw_centroids(key, part):
    values = shared_centroids(key, 1.6)
    return jnp.clip(values, -0.5, 0.5)


def draw_embeddings(key, part):
    own_key = jax.random.fold_in(key, 7)
    first, second, third, fourth = jax.random.split(own_key, 4)
    scales = jnp.exp(jax.random.uniform(first, (ROWS, 1), jnp.float32, jnp.log(0.5), jnp.log(5.0)))
    base = jax.random.truncated_normal(second, -4.0, 4.0, (ROWS, D), jnp.float32)
    values = base * scales * D ** (-0.5)
    centers = shared_centroids(key, 1.6)
    copies, taken = captured_rows(fourth, centers, 30.0, 60.0)
    values = jnp.where(taken[:, None], copies, values)
    return values.astype(jnp.bfloat16)


def setup_inputs(seed: int = 0) -> dict:
    keys = jax.random.split(jax.random.key(seed), 3)
    embeddings = draw_embeddings(jax.random.fold_in(keys[2], 71), 0)
    centroids = draw_centroids(jax.random.fold_in(keys[2], 71), 0)
    return dict(embeddings=embeddings, centroids=centroids)


logit_divisor = 0.05
prior = 0.5


def block_scores(embeddings, block):
    rounded = block.astype(jnp.bfloat16)
    pairwise_dots = jnp.dot(embeddings, rounded.T, preferred_element_type=jnp.float32)
    semi_length_energy = 0.5 * jnp.sum(block * block, axis=1)
    return (pairwise_dots - semi_length_energy[None, :]) / logit_divisor


def reference(embeddings, centroids):
    blocks = N_CENT
    width = K // blocks
    current = centroids
    log_total = jnp.zeros((ROWS,), jnp.float32)
    for step in range(ITERS):
        grouped = current.reshape(blocks, width, D)

        def gather_stats(carry, block):
            row_max, row_total = carry
            cluster_logits = block_scores(embeddings, block)
            top = jnp.maximum(row_max, jnp.max(cluster_logits, axis=1))
            row_total = row_total * jnp.exp(row_max - top) + jnp.sum(jnp.exp(cluster_logits - top[:, None]), axis=1)
            return (top, row_total), None

        start = (jnp.full((ROWS,), -jnp.inf, jnp.float32), jnp.zeros((ROWS,), jnp.float32))
        (row_max, row_total), unused = lax.scan(gather_stats, start, grouped)

        def update_block(block):
            cluster_logits = block_scores(embeddings, block)
            weights = (jnp.exp(cluster_logits - row_max[:, None]) / row_total[:, None]).astype(jnp.bfloat16)
            sums = lax.dot_general(weights, embeddings, (((0,), (0,)), ((), ())), preferred_element_type=jnp.float32)
            mass = jnp.sum(weights.astype(jnp.float32), axis=0)
            return (sums + prior * block) / (mass + prior)[:, None]

        current = lax.map(update_block, grouped).reshape(K, D)
        log_total = row_max + jnp.log(row_total)
    return current, log_total
```

```python
import jax
import jax.numpy as jnp
from jax import lax
from jax.experimental import pallas as pl
from jax.experimental.pallas import tpu as pltpu
from jax.sharding import PartitionSpec as P

MESH = pl.DeviceIdType.MESH
ITERS = 2
LOG2E = 1.4426950408889634
LN2 = 0.6931471805599453
SCALE = 20.0 * LOG2E
PRIOR = 0.5
D = 768
K = 1024
H = 512
R = 2048
UNIT = 256
PIECE = 32
STEPS = 16
CHUNK = 128
NT = (((1,), (1,)), ((), ()))


def place(x, y, z, core):
    x, y, z = lax.rem(x, 4), lax.rem(y, 4), lax.rem(z, 8)
    return (lax.rem(x, 2) * 2 + core, (z * 4 + y) * 2 + x // 2)


def kernel(
    e_hbm, c_hbm, out_c, out_l,
    e, land, sb, c, cb, nrm, p, ml, z1, z2, mid, tot, s, mass, rs, rsm, wbuf, d0, d1,
    esem, csem, osem, gsend, grecv, s1s, s1r, s2s, s2r, fs, fr, rss, rsr, ms, mr, ags, agr,
):
    dp, ct = lax.axis_index("dp"), lax.axis_index("cent")
    core, xlo = lax.rem(dp, 2), dp // 2
    xhi, y, z = lax.rem(ct, 2), lax.rem(ct // 2, 4), ct // 8
    x = xhi * 2 + xlo
    f1 = lax.rem(y + 2 * z, 4)
    f2 = lax.rem(z + 2 * y, 4)

    twin = place(x, y, z, 1 - core)
    xp, xm = place(x + 1, y, z, core), place(x + 3, y, z, core)
    yp, ym = place(x, y + 1, z, core), place(x, y + 3, z, core)
    zp, zm = place(x, y, z + 1, core), place(x, y, z + 7, core)
    partner = (lax.rem(dp + 2, 4), ct)
    zpeers = [place(x, y, z + k, core) for k in range(1, 8)]
    ypeers = [place(x, y + k, z, core) for k in range(1, 4)]
    ypeers += [place(x + 2, y + k, z, core) for k in range(4)]

    ecopy = pltpu.make_async_copy(e_hbm, e.at[pl.ds(0, R)], esem)
    ecopy.start()
    ccopy = pltpu.make_async_copy(c_hbm, c, csem)
    ccopy.start()

    barrier = pltpu.get_barrier_semaphore()
    peers = [twin, xp, xm] + zpeers + ypeers
    for peer in peers:
        pl.semaphore_signal(barrier, inc=1, device_id=peer, device_id_type=MESH)

    def rows(start, size):
        return pl.ds(pl.multiple_of(start, size), size)

    def remote(src, dst, ssem, rsem, to):
        return pltpu.make_async_remote_copy(
            src_ref=src, dst_ref=dst, send_sem=ssem, recv_sem=rsem, device_id=to, device_id_type=MESH
        )

    def unit_of(t):
        return jnp.where(t < 6, t, 7)

    def piece(u, half, q):
        return rows(u * UNIT + half * 128 + q * PIECE, PIECE)

    ecopy.wait()
    pl.semaphore_wait(barrier, len(peers))

    @pl.loop(0, 7)
    def _(t):
        u = unit_of(t)
        for half, q, to in ((0, f1, xm), (1, f2, xp)):
            src = sb.at[rows(t * 64 + half * 32, 32)]
            src[...] = e[piece(u, half, q), :].astype(jnp.float32)
            remote(
                src, land.at[piece(u, half, q)],
                gsend.at[42 + 2 * t + half], grecv.at[u * 8 + half * 4 + q], to,
            ).start()

    for half, to in ((0, xm), (1, xp)):
        src = sb.at[pl.ds(448 + half * 128, 128)]
        src[...] = e[pl.ds(6 * UNIT + half * 128, 128), :].astype(jnp.float32)
        remote(
            src, land.at[pl.ds(6 * UNIT + half * 128, 128)],
            gsend.at[56 + half], grecv.at[48 + half], to,
        ).start()

    def got(u, half, q):
        remote(
            land.at[piece(u, half, q)], land.at[piece(u, half, q)],
            gsend.at[0], grecv.at[u * 8 + half * 4 + q], twin,
        ).wait_recv()

    def forward(t):
        u = unit_of(t)
        odd = lax.rem(t, 2)
        got(u, 0, f1)
        got(u, 1, f2)
        zone = tuple(jnp.where(odd == 0, a, b) for a, b in zip(zp, zm))
        yone = tuple(jnp.where(odd == 0, a, b) for a, b in zip(yp, ym))
        sends = ((0, f1, yp), (1, f2, zp), (0, f1, ym), (1, f2, zm), (0, f1, zone), (1, f2, yone))
        for j, (half, q, to) in enumerate(sends):
            ref = land.at[piece(u, half, q)]
            remote(ref, ref, gsend.at[t * 6 + j], grecv.at[u * 8 + half * 4 + q], to).start()

    def arrive(u):
        @pl.when(u == 6)
        def _():
            for half in range(2):
                ref = land.at[pl.ds(6 * UNIT + half * 128, 128)]
                remote(ref, ref, gsend.at[0], grecv.at[48 + half], twin).wait_recv()

        @pl.when(u != 6)
        def _():
            for k in range(1, 4):
                got(u, 0, lax.rem(f1 + k, 4))
                got(u, 1, lax.rem(f2 + k, 4))

        e[rows(R + u * UNIT, UNIT), :] = land[rows(u * UNIT, UNIT), :].astype(jnp.bfloat16)

    ccopy.wait()

    def merge(ref, it):
        top = ref[it, 0, 0:8, :]
        for k in range(1, 8):
            top = jnp.maximum(top, ref[it, k, 0:8, :])
        total = jnp.zeros_like(top)
        for k in range(8):
            total += ref[it, k, 8:16, :] * jnp.exp2(ref[it, k, 0:8, :] - top)
        return top, total

    def stats_first(it):
        z1[it, z] = ml[0:16, :]
        for k, to in enumerate(zpeers):
            remote(z1.at[it, z], z1.at[it, z], s1s.at[it * 8 + k], s1r.at[it * 8 + z], to).start()

    def stats_second(it):
        for k in range(1, 8):
            src = lax.rem(z + k, 8)
            remote(z1.at[it, src], z1.at[it, src], s1s.at[0], s1r.at[it * 8 + src], twin).wait_recv()
        top, total = merge(z1, it)
        mid[it, 0:8, :] = top
        mid[it, 8:16, :] = total
        slot = y * 2 + xhi
        z2[it, slot] = mid[it]
        for k, to in enumerate(ypeers):
            remote(mid.at[it], z2.at[it, slot], s2s.at[it * 8 + k], s2r.at[it * 8 + slot], to).start()

    def stats_last(it):
        slot = y * 2 + xhi
        for k in range(1, 8):
            src = lax.rem(slot + k, 8)
            remote(z2.at[it, src], z2.at[it, src], s2s.at[0], s2r.at[it * 8 + src], twin).wait_recv()
        top, total = merge(z2, it)
        tot[it, 0:8, :] = top
        tot[it, 8:16, :] = total
        share(it).start()

    def share(it):
        return remote(tot.at[it, pl.ds(0, 16)], tot.at[it, pl.ds(16, 16)], fs.at[it], fr.at[it], partner)

    def prepare():
        @pl.loop(0, K // CHUNK)
        def _(k):
            at = rows(k * CHUNK, CHUNK)
            block = c[at, :]
            cb[at, :] = block.astype(jnp.bfloat16)
            nrm[at, :] = jnp.broadcast_to(0.5 * jnp.sum(block * block, axis=1, keepdims=True), (CHUNK, 128))

    def dot(u):
        return lax.dot_general(cb[...], e[rows(u * UNIT, UNIT), :], NT, preferred_element_type=jnp.float32)

    def soft(d, u):
        n = nrm[...]
        t = (d - jnp.concatenate([n, n], axis=1)) * SCALE
        m = jnp.max(t, axis=0, keepdims=True)
        w = jnp.exp2(t - m)
        p[u] = w
        at = (u // 8) * 16 + lax.rem(u, 8)
        ml[pl.ds(at, 1), :] = m
        ml[pl.ds(at + 8, 1), :] = jnp.sum(w, axis=0, keepdims=True)

    def scores(g):
        d0[...] = dot(2 * g)
        d1[...] = dot(2 * g + 1)
        soft(d0[...], 2 * g)
        soft(d1[...], 2 * g + 1)

    def weigh(g, it):
        side = g // 4

        @pl.when(lax.rem(g, 4) == 0)
        def _():
            s[side] = jnp.zeros((K, D), jnp.float32)
            mass[side] = jnp.zeros((K, 128), jnp.float32)

        total = mass[side]
        for j in range(2):
            at = side * 16 + lax.rem(2 * g, 8) + j
            part = jnp.exp2(ml[pl.ds(at, 1), :] - tot[it, pl.ds(at, 1), :]) / tot[it, pl.ds(at + 8, 1), :]
            w = (p[2 * g + j] * part).astype(jnp.bfloat16)
            wide = w.astype(jnp.float32)
            total += wide[:, :128] + wide[:, 128:]
            wbuf[:, j * UNIT : (j + 1) * UNIT] = w
        mass[side] = total
        s[side] += jnp.dot(wbuf[...], e[rows(g * 512, 512), :], preferred_element_type=jnp.float32)

    def update(it):
        mine, theirs = core * H, (1 - core) * H
        n = H // CHUNK

        @pl.loop(0, n)
        def _(k):
            at = rows(theirs + k * CHUNK, CHUNK)
            to = rows(k * CHUNK, CHUNK)
            s[0, at, :] += s[1, at, :]
            mass[0, at, :] += mass[1, at, :]
            remote(s.at[0, at], rs.at[to], rss.at[it * n + k], rsr.at[it * n + k], twin).start()
            remote(mass.at[0, at], rsm.at[to], ms.at[it * n + k], mr.at[it * n + k], twin).start()

        @pl.loop(0, n)
        def _(k):
            at = rows(mine + k * CHUNK, CHUNK)
            to = rows(k * CHUNK, CHUNK)
            remote(s.at[0, at], rs.at[to], rss.at[it * n + k], rsr.at[it * n + k], twin).wait_recv()
            remote(mass.at[0, at], rsm.at[to], ms.at[it * n + k], mr.at[it * n + k], twin).wait_recv()
            full = (mass[0, at, :] + mass[1, at, :]) + rsm[to, :]
            scale = 1.0 / (jnp.sum(full, axis=1, keepdims=True) + PRIOR)
            c[at, :] = ((s[0, at, :] + s[1, at, :]) + rs[to, :] + PRIOR * c[at, :]) * scale

            @pl.when(it == 0)
            def _():
                remote(c.at[at], c.at[at], ags.at[k], agr.at[k], twin).start()

            @pl.when(it == 1)
            def _():
                remote(c.at[at], out_c.at[at], ags.at[n + k], agr.at[n + k], twin).start()
                pltpu.make_async_copy(c.at[at], out_c.at[at], osem.at[k]).start()

        @pl.loop(0, n)
        def _(k):
            at = rows(theirs + k * CHUNK, CHUNK)
            to = rows(k * CHUNK, CHUNK)
            remote(s.at[0, at], rs.at[to], rss.at[it * n + k], rsr.at[it * n + k], twin).wait_send()
            remote(mass.at[0, at], rsm.at[to], ms.at[it * n + k], mr.at[it * n + k], twin).wait_send()

            @pl.when(it == 0)
            def _():
                remote(c.at[at], c.at[at], ags.at[k], agr.at[k], twin).wait()

            @pl.when(it == 1)
            def _():
                remote(c.at[at], out_c.at[at], ags.at[n + k], agr.at[n + k], twin).wait()
                pltpu.make_async_copy(c.at[at], out_c.at[at], osem.at[k]).wait()

    @pl.loop(0, ITERS * STEPS)
    def _(step):
        it, r = step // STEPS, lax.rem(step, STEPS)
        first = it == 0
        late = jnp.logical_and(first, r >= 12)
        split = jnp.where(first, 6, 8)
        is_scores = jnp.where(late, lax.rem(r, 2) == 0, r < split)
        g = jnp.where(late, 6 + (r - 12) // 2, jnp.where(r < split, r, r - split))

        def at(cond):
            return pl.when(cond)

        @at(r == 0)
        def _():
            prepare()

        @at(jnp.logical_and(first, jnp.logical_or(r == 2, r == 3)))
        def _():
            forward(r - 2)

        @at(r == 4)
        def _():
            stats_first(it)

        @at(jnp.logical_and(first, jnp.logical_or(r == 4, r == 5)))
        def _():
            forward(2 * r - 6)

        @at(r == jnp.where(first, 5, 6))
        def _():
            stats_second(it)

        @at(jnp.logical_and(first, jnp.logical_or(r == 4, r == 5)))
        def _():
            forward(2 * r - 5)

        @at(jnp.logical_and(first, r == 5))
        def _():
            forward(6)

        @at(jnp.logical_and(jnp.logical_and(first, is_scores), g >= 4))
        def _():
            arrive(2 * g - 8)
            arrive(2 * g - 7)

        @at(r == jnp.where(first, 6, 8))
        def _():
            stats_last(it)

        @at(r == jnp.where(first, 10, 12))
        def _():
            share(it).wait_recv()

        @at(is_scores)
        def _():
            scores(g)

        @at(jnp.logical_not(is_scores))
        def _():
            weigh(g, it)

        @at(r == STEPS - 1)
        def _():
            update(it)

    @pl.loop(0, 56)
    def _(k):
        ref = land.at[pl.ds(0, PIECE)]
        remote(ref, ref, gsend.at[k], grecv.at[0], twin).wait_send()

    for half in range(2):
        ref = land.at[pl.ds(0, 128)]
        remote(ref, ref, gsend.at[56 + half], grecv.at[0], twin).wait_send()

    for it in range(ITERS):
        for k in range(7):
            ref = mid.at[0]
            remote(ref, ref, s1s.at[it * 8 + k], s1r.at[0], twin).wait_send()
            remote(ref, ref, s2s.at[it * 8 + k], s2r.at[0], twin).wait_send()
        share(it).wait_send()

    value = (tot[1, 0:8, :] + jnp.log2(tot[1, 8:16, :])) * LN2
    for u in range(8):
        out_l[2 * u : 2 * u + 1, :] = value[u : u + 1, :128]
        out_l[2 * u + 1 : 2 * u + 2, :] = value[u : u + 1, 128:]


def local(embeddings, centroids):
    f32, bf16, dma = jnp.float32, jnp.bfloat16, pltpu.SemaphoreType.DMA
    vmem = pltpu.VMEM
    new, logs = pl.pallas_call(
        kernel,
        out_shape=(jax.ShapeDtypeStruct((K, D), f32), jax.ShapeDtypeStruct((16, 128), f32)),
        in_specs=[pl.BlockSpec(memory_space=pl.ANY)] * 2,
        out_specs=(pl.BlockSpec(memory_space=pl.ANY), pl.BlockSpec(memory_space=pltpu.VMEM)),
        scratch_shapes=[
            vmem((2 * R, D), bf16),
            vmem((R, D), f32),
            vmem((704, D), f32),
            vmem((K, D), f32),
            vmem((K, D), bf16),
            vmem((K, 128), f32),
            vmem((16, K, UNIT), f32),
            vmem((32, UNIT), f32),
            vmem((2, 8, 16, UNIT), f32),
            vmem((2, 8, 16, UNIT), f32),
            vmem((2, 16, UNIT), f32),
            vmem((2, 32, UNIT), f32),
            vmem((2, K, D), f32),
            vmem((2, K, 128), f32),
            vmem((H, D), f32),
            vmem((H, 128), f32),
            vmem((K, 2 * UNIT), bf16),
            vmem((K, UNIT), f32),
            vmem((K, UNIT), f32),
            dma, dma, dma((4,)),
            dma((64,)), dma((64,)),
            dma((16,)), dma((16,)), dma((16,)), dma((16,)),
            dma((2,)), dma((2,)),
            dma((8,)), dma((8,)), dma((8,)), dma((8,)), dma((8,)), dma((8,)),
        ],
        compiler_params=pltpu.CompilerParams(
            collective_id=0, has_side_effects=True, vmem_limit_bytes=60 << 20
        ),
    )(embeddings, centroids)
    return new, logs.reshape(R)


def solution(mesh):
    placed = (P("dp", None), P("cent", None))
    return jax.shard_map(
        local, mesh=mesh, in_specs=placed, out_specs=(P("cent", None), P("dp")), check_vma=False
    )
```

```python
import jax
import jax.numpy as jnp
from jax import lax
from jax.experimental import pallas as pl
from jax.experimental.pallas import tpu as pltpu
from jax.sharding import PartitionSpec as P

MESH = pl.DeviceIdType.MESH
ITERS = 2
LOG2E = 1.4426950408889634
LN2 = 0.6931471805599453
SCALE = 20.0 * LOG2E
PRIOR = 0.5
D = 768
K = 1024
H = 512
R = 2048
UNIT = 256
PIECE = 32
CHUNK = 128
BLOCK = 256
NT = (((1,), (1,)), ((), ()))


def place(x, y, z, core):
    x, y, z = lax.rem(x, 4), lax.rem(y, 4), lax.rem(z, 8)
    return (lax.rem(x, 2) * 2 + core, (z * 4 + y) * 2 + x // 2)


def kernel(
    e_hbm, c_hbm, out_c, out_t,
    e, land, sb, c, cb, nrm, p, ml, z1, z2, tot, s, mass, rs, rsm, wbuf, d0, d1,
    esem, csem, osem, gsend, grecv, s1s, s1r, s2s, s2r, fs, fr, rss, rsr, ms, mr, ags, agr, relay,
):
    dp, ct = lax.axis_index("dp"), lax.axis_index("cent")
    core, xlo = lax.rem(dp, 2), dp // 2
    xhi, y, z = lax.rem(ct, 2), lax.rem(ct // 2, 4), ct // 8
    x = xhi * 2 + xlo
    f1 = lax.rem(y + 2 * z, 4)
    f2 = lax.rem(z + 2 * y, 4)

    twin = place(x, y, z, 1 - core)
    xp, xm = place(x + 1, y, z, core), place(x + 3, y, z, core)
    yp, ym = place(x, y + 1, z, core), place(x, y + 3, z, core)
    zp, zm = place(x, y, z + 1, core), place(x, y, z + 7, core)
    partner = (lax.rem(dp + 2, 4), ct)
    zpeers = [place(x, y, z + k, core) for k in range(1, 8)]
    ypeers = [place(x, y + k, z, core) for k in range(1, 4)]
    ypeers += [place(x + 2, y + k, z, core) for k in range(4)]

    ecopy = pltpu.make_async_copy(e_hbm, e.at[pl.ds(0, R)], esem)
    ecopy.start()
    ccopy = pltpu.make_async_copy(c_hbm, c, csem)
    ccopy.start()

    barrier = pltpu.get_barrier_semaphore()
    near = [xp, xm, yp, ym, zp, zm]
    for peer in near + [twin]:
        pl.semaphore_signal(barrier, inc=1, device_id=peer, device_id_type=MESH)

    def rows(start, size):
        return pl.ds(pl.multiple_of(start, size), size)

    def remote(src, dst, ssem, rsem, to):
        return pltpu.make_async_remote_copy(
            src_ref=src, dst_ref=dst, send_sem=ssem, recv_sem=rsem, device_id=to, device_id_type=MESH
        )

    def unit_of(t):
        return jnp.where(t < 6, t, 7)

    def piece(u, half, q):
        return rows(u * UNIT + half * 128 + q * PIECE, PIECE)

    ecopy.wait()
    pl.semaphore_wait(barrier, 7)

    def tell(r):
        for peer in near:
            pl.semaphore_signal(relay.at[r], inc=1, device_id=peer, device_id_type=MESH)

    def told(r):
        pl.semaphore_wait(relay.at[r], 6)

    def spread(t):
        u = unit_of(t)
        for half, q, to in ((0, f1, xm), (1, f2, xp)):
            src = sb.at[rows(t * 64 + half * 32, 32)]
            src[...] = e[piece(u, half, q), :].astype(jnp.float32)
            remote(
                src, land.at[piece(u, half, q)],
                gsend.at[42 + 2 * t + half], grecv.at[u * 8 + half * 4 + q], to,
            ).start()

        @pl.when(t == 6)
        def _():
            for half, q, to in ((0, f1 + 2, xm), (1, f2 + 2, xp)):
                q = lax.rem(q, 4)
                src = sb.at[rows(704 + half * 32, 32)]
                src[...] = e[piece(7, half, q), :].astype(jnp.float32)
                remote(
                    src, land.at[piece(7, half, q)], gsend.at[40 + half], grecv.at[56 + half * 4 + q], to
                ).start()

    def spread_whole():
        for half, to in ((0, xm), (1, xp)):
            src = sb.at[pl.ds(448 + half * 128, 128)]
            src[...] = e[pl.ds(6 * UNIT + half * 128, 128), :].astype(jnp.float32)
            remote(
                src, land.at[pl.ds(6 * UNIT + half * 128, 128)],
                gsend.at[56 + half], grecv.at[48 + half], to,
            ).start()

    spread(0)
    tell(0)

    @pl.loop(1, 7)
    def _(t):
        spread(t)

    spread_whole()

    def got(u, half, q):
        remote(
            land.at[piece(u, half, q)], land.at[piece(u, half, q)],
            gsend.at[0], grecv.at[u * 8 + half * 4 + q], twin,
        ).wait_recv()

    def forward(t):
        u = unit_of(t)
        odd = lax.rem(t, 2)
        got(u, 0, f1)
        got(u, 1, f2)
        zone = tuple(jnp.where(odd == 0, a, b) for a, b in zip(zp, zm))
        yone = tuple(jnp.where(odd == 0, a, b) for a, b in zip(yp, ym))
        sends = ((0, f1, yp), (1, f2, zp), (0, f1, ym), (1, f2, zm), (0, f1, zone), (1, f2, yone))

        def send(j):
            half, q, to = sends[j]
            ref = land.at[piece(u, half, q)]
            remote(ref, ref, gsend.at[t * 6 + j], grecv.at[u * 8 + half * 4 + q], to).start()

        for j in range(4):
            send(j)

        @pl.when(t < 6)
        def _():
            send(4)
            send(5)


    def arrive(u):
        @pl.when(u == 6)
        def _():
            for half in range(2):
                ref = land.at[pl.ds(6 * UNIT + half * 128, 128)]
                remote(ref, ref, gsend.at[0], grecv.at[48 + half], twin).wait_recv()

        @pl.when(u != 6)
        def _():
            for k in range(1, 4):
                got(u, 0, lax.rem(f1 + k, 4))
                got(u, 1, lax.rem(f2 + k, 4))

        e[rows(R + u * UNIT, UNIT), :] = land[rows(u * UNIT, UNIT), :].astype(jnp.bfloat16)

    ccopy.wait()

    def prepare(at):
        block = c[at, :]
        cb[at, :] = block.astype(jnp.bfloat16)
        nrm[at, :] = jnp.broadcast_to(0.5 * jnp.sum(block * block, axis=1, keepdims=True), (CHUNK, 128))

    def merge(ref, it, h):
        top = ref[it, h, 0, 0:4, :]
        for k in range(1, 8):
            top = jnp.maximum(top, ref[it, h, k, 0:4, :])
        total = jnp.zeros_like(top)
        for k in range(8):
            total += ref[it, h, k, 4:8, :] * jnp.exp2(ref[it, h, k, 0:4, :] - top)
        return top, total

    def send_all(ref, it, h, slot, ssem, rsem, peers):
        for k, to in enumerate(peers):
            at = (it * 2 + h) * 8
            remote(ref.at[it, h, slot], ref.at[it, h, slot], ssem.at[at + k], rsem.at[at + slot], to).start()

    def receive_all(ref, it, h, slot, ssem, rsem):
        for k in range(1, 8):
            src = lax.rem(slot + k, 8)
            at = (it * 2 + h) * 8 + src
            remote(ref.at[it, h, src], ref.at[it, h, src], ssem.at[0], rsem.at[at], twin).wait_recv()

    def stats_first(it, h):
        z1[it, h, z] = ml[h * 8 : h * 8 + 8, :]
        send_all(z1, it, h, z, s1s, s1r, zpeers)

    yslot = y * 2 + xhi

    def stats_second(it, h):
        receive_all(z1, it, h, z, s1s, s1r)
        top, total = merge(z1, it, h)
        z2[it, h, yslot, 0:4, :] = top
        z2[it, h, yslot, 4:8, :] = total
        send_all(z2, it, h, yslot, s2s, s2r, ypeers)

    def share(it, h):
        src, dst = tot.at[it, pl.ds(h * 8, 8)], tot.at[it, pl.ds(16 + h * 8, 8)]
        return remote(src, dst, fs.at[it * 2 + h], fr.at[it * 2 + h], partner)

    def stats_last(it, h):
        receive_all(z2, it, h, yslot, s2s, s2r)
        top, total = merge(z2, it, h)
        tot[it, h * 8 : h * 8 + 4, :] = top
        tot[it, h * 8 + 4 : h * 8 + 8, :] = total
        share(it, h).start()

    def dot(g):
        return lax.dot_general(cb[...], e[rows(g * 512, 512), :], NT, preferred_element_type=jnp.float32)

    def stat_row(u):
        return (u // 4) * 8 + lax.rem(u, 4)

    def soft(d, g):
        n = nrm[...]
        n = jnp.concatenate([n, n], axis=1)
        for j in range(2):
            u = 2 * g + j
            t = (d[:, j * UNIT : (j + 1) * UNIT] - n) * SCALE
            m = jnp.max(t, axis=0, keepdims=True)
            w = jnp.exp2(t - m)
            p[u] = w
            ml[pl.ds(stat_row(u), 1), :] = m
            ml[pl.ds(stat_row(u) + 4, 1), :] = jnp.sum(w, axis=0, keepdims=True)

    def scores(g):
        d0[...] = dot(g)
        soft(d0, g)

    def weigh(it, u0, n, at):
        total = jnp.zeros((BLOCK, 128), jnp.float32)
        for j in range(n):
            row = stat_row(u0 + j)
            part = jnp.exp2(ml[pl.ds(row, 1), :] - tot[it, pl.ds(row, 1), :]) / tot[it, pl.ds(row + 4, 1), :]
            w = (p[u0 + j, at, :] * part).astype(jnp.bfloat16)
            wide = w.astype(jnp.float32)
            total += wide[:, :128] + wide[:, 128:]
            wbuf[:, j * UNIT : (j + 1) * UNIT] = w
        block = e[rows(u0 * UNIT, n * UNIT), :]
        return jnp.dot(wbuf[:, : n * UNIT], block, preferred_element_type=jnp.float32), total

    def weigh_half(it, side, h, at):
        add, total = weigh(it, 8 * side + 4 * h, 4, at)
        s[side, at, :] = add if h == 0 else s[side, at, :] + add
        mass[side, at, :] = total if h == 0 else mass[side, at, :] + total

    def weigh_own(it, h):
        @pl.loop(0, K // BLOCK)
        def _(k):
            weigh_half(it, 0, h, rows(k * BLOCK, BLOCK))

    mine, theirs = core * H, (1 - core) * H
    n = H // BLOCK

    def update(it):
        def finish_sums(at):
            for h in range(2):
                weigh_half(it, 1, h, at)
            return s[0, at, :] + s[1, at, :], mass[0, at, :] + mass[1, at, :]

        def give(k):
            at, to = rows(theirs + k * BLOCK, BLOCK), rows(k * BLOCK, BLOCK)
            i = it * n + k
            return (
                remote(s.at[0, at], rs.at[to], rss.at[i], rsr.at[i], twin),
                remote(mass.at[0, at], rsm.at[to], ms.at[i], mr.at[i], twin),
            )

        def spread_new(start, i):
            at = rows(start + i * CHUNK, CHUNK)
            dst = c if it == 0 else out_c
            return remote(c.at[at], dst.at[at], ags.at[it * 4 + i], agr.at[it * 4 + i], twin)

        @pl.loop(0, n)
        def _(k):
            at = rows(theirs + k * BLOCK, BLOCK)
            sums, total = finish_sums(at)
            s[0, at, :] = sums
            mass[0, at, :] = total
            for copy in give(k):
                copy.start()

        @pl.loop(0, n)
        def _(k):
            at, to = rows(mine + k * BLOCK, BLOCK), rows(k * BLOCK, BLOCK)
            sums, total = finish_sums(at)
            for copy in give(k):
                copy.wait_recv()
            total = total + rsm[to, :]
            scale = 1.0 / (jnp.sum(total, axis=1, keepdims=True) + PRIOR)
            for j in range(BLOCK // CHUNK):
                sub = rows(mine + k * BLOCK + j * CHUNK, CHUNK)
                cut = slice(j * CHUNK, (j + 1) * CHUNK)
                add = rs[rows(k * BLOCK + j * CHUNK, CHUNK), :]
                c[sub, :] = (sums[cut, :] + add + PRIOR * c[sub, :]) * scale[cut, :]
                spread_new(mine, 2 * k + j).start()
                if it == 0:
                    prepare(sub)
            if it == 1:
                pltpu.make_async_copy(c.at[at], out_c.at[at], osem.at[k]).start()

        @pl.loop(0, n)
        def _(k):
            for copy in give(k):
                copy.wait_send()
            for j in range(BLOCK // CHUNK):
                spread_new(theirs, 2 * k + j).wait()
                if it == 0:
                    prepare(rows(theirs + k * BLOCK + j * CHUNK, CHUNK))
            if it == 1:
                at = rows(mine + k * BLOCK, BLOCK)
                pltpu.make_async_copy(c.at[at], out_c.at[at], osem.at[k]).wait()

    def pipelined(pairs, hook):
        d0[...] = dot(0)

        @pl.loop(0, pairs)
        def _(k):
            d1[...] = dot(2 * k + 1)
            soft(d0, 2 * k)

            @pl.when(k < pairs - 1)
            def _():
                d0[...] = dot(2 * k + 2)
                soft(d1, 2 * k + 1)

            @pl.when(k == pairs - 1)
            def _():
                soft(d1, 2 * pairs - 1)

            hook(k)

    @pl.loop(0, K // CHUNK)
    def _(k):
        prepare(rows(k * CHUNK, CHUNK))

    def meanwhile(k):
        @pl.when(k == 0)
        def _():
            told(0)
            tell(1)

        @pl.when(k == 1)
        def _():
            told(1)
            tell(2)

        forward(k)

    pipelined(2, meanwhile)
    forward(2)
    told(2)
    for h in range(2):
        stats_first(0, h)
    for t in (3, 4):
        forward(t)

    @pl.loop(4, 8)
    def _(g):
        arrive(2 * g - 8)
        arrive(2 * g - 7)
        scores(g)

        @pl.when(g == 4)
        def _():
            for h in range(2):
                stats_second(0, h)

            @pl.loop(5, 7)
            def _(t):
                forward(t)

            for h in range(2):
                stats_last(0, h)
                weigh_own(0, h)

    for h in range(2):
        share(0, h).wait_recv()
    update(0)

    def between(k):
        for h in range(2):

            @pl.when(k == h)
            def _():
                stats_first(1, h)

        @pl.when(k == 2)
        def _():
            stats_second(1, 0)

    pipelined(4, between)
    stats_second(1, 1)
    for h in range(2):
        stats_last(1, h)
        weigh_own(1, h)
    for h in range(2):
        share(1, h).wait_recv()
    update(1)

    @pl.loop(0, 56)
    def _(k):
        ref = land.at[pl.ds(0, PIECE)]
        remote(ref, ref, gsend.at[k], grecv.at[0], twin).wait_send()

    for half in range(2):
        ref = land.at[pl.ds(0, 128)]
        remote(ref, ref, gsend.at[56 + half], grecv.at[0], twin).wait_send()

    for it in range(ITERS):
        for h in range(2):
            ref = z1.at[0, 0, 0]
            for k in range(7):
                remote(ref, ref, s1s.at[(it * 2 + h) * 8 + k], s1r.at[0], twin).wait_send()
                remote(ref, ref, s2s.at[(it * 2 + h) * 8 + k], s2r.at[0], twin).wait_send()
            share(it, h).wait_send()

    out_t[...] = tot[1, 0:16, :]


def finish(c, tot, out_c, out_l, sems):
    copies = []
    for k in range(8):
        at = pl.ds(k * 128, 128)
        copies.append(pltpu.make_async_copy(c.at[at], out_c.at[at], sems.at[k]))
        copies[k].start()
    for h in range(2):
        value = (tot[h * 8 : h * 8 + 4, :] + jnp.log2(tot[h * 8 + 4 : h * 8 + 8, :])) * LN2
        for j in range(4):
            at = 8 * h + 2 * j
            out_l[at : at + 1, :] = value[j : j + 1, :128]
            out_l[at + 1 : at + 2, :] = value[j : j + 1, 128:]
    for copy in copies:
        copy.wait()


def local(embeddings, centroids):
    f32, bf16, dma = jnp.float32, jnp.bfloat16, pltpu.SemaphoreType.DMA
    vmem = pltpu.VMEM
    new, stats = pl.pallas_call(
        kernel,
        out_shape=(jax.ShapeDtypeStruct((K, D), f32), jax.ShapeDtypeStruct((16, UNIT), f32)),
        in_specs=[pl.BlockSpec(memory_space=pl.ANY)] * 2,
        out_specs=(pl.BlockSpec(memory_space=pl.ANY), pl.BlockSpec(memory_space=pltpu.VMEM)),
        scratch_shapes=[
            vmem((2 * R, D), bf16),
            vmem((R, D), f32),
            vmem((768, D), f32),
            vmem((K, D), f32),
            vmem((K, D), bf16),
            vmem((K, 128), f32),
            vmem((16, K, UNIT), f32),
            vmem((32, UNIT), f32),
            vmem((2, 2, 8, 8, UNIT), f32),
            vmem((2, 2, 8, 8, UNIT), f32),
            vmem((2, 32, UNIT), f32),
            vmem((2, K, D), f32),
            vmem((2, K, 128), f32),
            vmem((H, D), f32),
            vmem((H, 128), f32),
            vmem((BLOCK, 4 * UNIT), bf16),
            vmem((K, 2 * UNIT), f32),
            vmem((K, 2 * UNIT), f32),
            dma, dma, dma((4,)),
            dma((64,)), dma((64,)),
            dma((32,)), dma((32,)), dma((32,)), dma((32,)),
            dma((4,)), dma((4,)),
            dma((4,)), dma((4,)), dma((4,)), dma((4,)), dma((8,)), dma((8,)),
            pltpu.SemaphoreType.REGULAR((3,)),
        ],
        compiler_params=pltpu.CompilerParams(
            collective_id=0, has_side_effects=True, vmem_limit_bytes=54 << 20
        ),
    )(embeddings, centroids)
    new, logs = pl.pallas_call(
        finish,
        out_shape=(jax.ShapeDtypeStruct((K, D), f32), jax.ShapeDtypeStruct((16, 128), f32)),
        in_specs=[pl.BlockSpec(memory_space=pl.ANY), pl.BlockSpec(memory_space=vmem)],
        out_specs=(pl.BlockSpec(memory_space=pl.ANY), pl.BlockSpec(memory_space=vmem)),
        scratch_shapes=[dma((8,))],
        compiler_params=pltpu.CompilerParams(vmem_limit_bytes=60 << 20),
    )(new, stats)
    return new, logs.reshape(R)


def solution(mesh):
    placed = (P("dp", None), P("cent", None))
    return jax.shard_map(
        local, mesh=mesh, in_specs=placed, out_specs=(P("cent", None), P("dp")), check_vma=False
    )
```

```python
import jax
import jax.numpy as jnp
from jax import lax
from jax.experimental import pallas as pl
from jax.experimental.pallas import tpu as pltpu
from jax.sharding import PartitionSpec as P

MESH = pl.DeviceIdType.MESH
ITERS = 2
LOG2E = 1.4426950408889634
LN2 = 0.6931471805599453
SCALE = 20.0 * LOG2E
PRIOR = 0.5
D = 768
K = 1024
H = 512
R = 2048
UNIT = 256
PIECE = 32
CHUNK = 128
BLOCK = 256
NT = (((1,), (1,)), ((), ()))


def place(x, y, z, core):
    x, y, z = lax.rem(x, 4), lax.rem(y, 4), lax.rem(z, 8)
    return (lax.rem(x, 2) * 2 + core, (z * 4 + y) * 2 + x // 2)


def kernel(
    e_hbm, c_hbm, out_c, out_t,
    e, land, sb, c, cb, nrm, p, ml, z1, z2, tot, s, mass, rs, rsm, wbuf, d0, d1,
    esem, csem, osem, gsend, grecv, s1s, s1r, s2s, s2r, fs, fr, rss, rsr, ms, mr, ags, agr, relay,
):
    dp, ct = lax.axis_index("dp"), lax.axis_index("cent")
    core, xlo = lax.rem(dp, 2), dp // 2
    xhi, y, z = lax.rem(ct, 2), lax.rem(ct // 2, 4), ct // 8
    x = xhi * 2 + xlo
    f1 = lax.rem(y + 2 * z, 4)
    f2 = lax.rem(z + 2 * y, 4)

    twin = place(x, y, z, 1 - core)
    xp, xm = place(x + 1, y, z, core), place(x + 3, y, z, core)
    yp, ym = place(x, y + 1, z, core), place(x, y + 3, z, core)
    zp, zm = place(x, y, z + 1, core), place(x, y, z + 7, core)
    partner = (lax.rem(dp + 2, 4), ct)
    zpeers = [place(x, y, z + k, core) for k in range(1, 8)]
    ypeers = [place(x, y + k, z, core) for k in range(1, 4)]
    ypeers += [place(x + 2, y + k, z, core) for k in range(4)]

    ecopy = pltpu.make_async_copy(e_hbm, e.at[pl.ds(0, R)], esem)
    ecopy.start()
    ccopy = pltpu.make_async_copy(c_hbm, c, csem)
    ccopy.start()

    barrier = pltpu.get_barrier_semaphore()
    near = [xp, xm, yp, ym, zp, zm]
    for peer in near + [twin]:
        pl.semaphore_signal(barrier, inc=1, device_id=peer, device_id_type=MESH)

    def rows(start, size):
        return pl.ds(pl.multiple_of(start, size), size)

    def remote(src, dst, ssem, rsem, to):
        return pltpu.make_async_remote_copy(
            src_ref=src, dst_ref=dst, send_sem=ssem, recv_sem=rsem, device_id=to, device_id_type=MESH
        )

    def unit_of(t):
        return jnp.where(t < 6, t, 7)

    def piece(u, half, q):
        return rows(u * UNIT + half * 128 + q * PIECE, PIECE)

    ecopy.wait()
    pl.semaphore_wait(barrier, 7)

    def tell(r):
        for peer in near:
            pl.semaphore_signal(relay.at[r], inc=1, device_id=peer, device_id_type=MESH)

    def told(r):
        pl.semaphore_wait(relay.at[r], 6)

    def spread(t):
        u = unit_of(t)
        for half, q, to in ((0, f1, xm), (1, f2, xp)):
            src = sb.at[rows(t * 64 + half * 32, 32)]
            src[...] = e[piece(u, half, q), :].astype(jnp.float32)
            remote(
                src, land.at[piece(u, half, q)],
                gsend.at[42 + 2 * t + half], grecv.at[u * 8 + half * 4 + q], to,
            ).start()

        @pl.when(t == 6)
        def _():
            for half, q, to in ((0, f1 + 2, xm), (1, f2 + 2, xp)):
                q = lax.rem(q, 4)
                src = sb.at[rows(704 + half * 32, 32)]
                src[...] = e[piece(7, half, q), :].astype(jnp.float32)
                remote(
                    src, land.at[piece(7, half, q)], gsend.at[40 + half], grecv.at[56 + half * 4 + q], to
                ).start()

    def spread_whole():
        for half, to in ((0, xm), (1, xp)):
            src = sb.at[pl.ds(448 + half * 128, 128)]
            src[...] = e[pl.ds(6 * UNIT + half * 128, 128), :].astype(jnp.float32)
            remote(
                src, land.at[pl.ds(6 * UNIT + half * 128, 128)],
                gsend.at[56 + half], grecv.at[48 + half], to,
            ).start()

    spread(0)
    tell(0)

    spread(1)

    def got(u, half, q):
        remote(
            land.at[piece(u, half, q)], land.at[piece(u, half, q)],
            gsend.at[0], grecv.at[u * 8 + half * 4 + q], twin,
        ).wait_recv()

    def forward(t):
        u = unit_of(t)
        odd = lax.rem(t, 2)
        got(u, 0, f1)
        got(u, 1, f2)
        zone = tuple(jnp.where(odd == 0, a, b) for a, b in zip(zp, zm))
        yone = tuple(jnp.where(odd == 0, a, b) for a, b in zip(yp, ym))
        sends = ((0, f1, yp), (1, f2, zp), (0, f1, ym), (1, f2, zm), (0, f1, zone), (1, f2, yone))

        def send(j):
            half, q, to = sends[j]
            ref = land.at[piece(u, half, q)]
            remote(ref, ref, gsend.at[t * 6 + j], grecv.at[u * 8 + half * 4 + q], to).start()

        for j in range(4):
            send(j)

        @pl.when(t < 6)
        def _():
            send(4)
            send(5)


    def arrive(u):
        @pl.when(u == 6)
        def _():
            for half in range(2):
                ref = land.at[pl.ds(6 * UNIT + half * 128, 128)]
                remote(ref, ref, gsend.at[0], grecv.at[48 + half], twin).wait_recv()

        @pl.when(u != 6)
        def _():
            for k in range(1, 4):
                got(u, 0, lax.rem(f1 + k, 4))
                got(u, 1, lax.rem(f2 + k, 4))

        e[rows(R + u * UNIT, UNIT), :] = land[rows(u * UNIT, UNIT), :].astype(jnp.bfloat16)

    ccopy.wait()

    def prepare(at):
        block = c[at, :]
        cb[at, :] = block.astype(jnp.bfloat16)
        nrm[at, :] = jnp.broadcast_to(0.5 * jnp.sum(block * block, axis=1, keepdims=True), (CHUNK, 128))

    def merge(ref, it, h):
        top = ref[it, h, 0, 0:4, :]
        for k in range(1, 8):
            top = jnp.maximum(top, ref[it, h, k, 0:4, :])
        total = jnp.zeros_like(top)
        for k in range(8):
            total += ref[it, h, k, 4:8, :] * jnp.exp2(ref[it, h, k, 0:4, :] - top)
        return top, total

    def send_all(ref, it, h, slot, ssem, rsem, peers):
        for k, to in enumerate(peers):
            at = (it * 2 + h) * 8
            remote(ref.at[it, h, slot], ref.at[it, h, slot], ssem.at[at + k], rsem.at[at + slot], to).start()

    def receive_all(ref, it, h, slot, ssem, rsem):
        for k in range(1, 8):
            src = lax.rem(slot + k, 8)
            at = (it * 2 + h) * 8 + src
            remote(ref.at[it, h, src], ref.at[it, h, src], ssem.at[0], rsem.at[at], twin).wait_recv()

    def stats_first(it, h):
        z1[it, h, z] = ml[h * 8 : h * 8 + 8, :]
        send_all(z1, it, h, z, s1s, s1r, zpeers)

    yslot = y * 2 + xhi

    def stats_second(it, h):
        receive_all(z1, it, h, z, s1s, s1r)
        top, total = merge(z1, it, h)
        z2[it, h, yslot, 0:4, :] = top
        z2[it, h, yslot, 4:8, :] = total
        send_all(z2, it, h, yslot, s2s, s2r, ypeers)

    def share(it, h):
        src, dst = tot.at[it, pl.ds(h * 8, 8)], tot.at[it, pl.ds(16 + h * 8, 8)]
        return remote(src, dst, fs.at[it * 2 + h], fr.at[it * 2 + h], partner)

    def stats_last(it, h):
        receive_all(z2, it, h, yslot, s2s, s2r)
        top, total = merge(z2, it, h)
        tot[it, h * 8 : h * 8 + 4, :] = top
        tot[it, h * 8 + 4 : h * 8 + 8, :] = total
        share(it, h).start()

    def dot(g):
        return lax.dot_general(cb[...], e[rows(g * 512, 512), :], NT, preferred_element_type=jnp.float32)

    def stat_row(u):
        return (u // 4) * 8 + lax.rem(u, 4)

    def soft(d, g):
        n = nrm[...]
        n = jnp.concatenate([n, n], axis=1)
        for j in range(2):
            u = 2 * g + j
            t = (d[:, j * UNIT : (j + 1) * UNIT] - n) * SCALE
            m = jnp.max(t, axis=0, keepdims=True)
            w = jnp.exp2(t - m)
            p[u] = w
            ml[pl.ds(stat_row(u), 1), :] = m
            ml[pl.ds(stat_row(u) + 4, 1), :] = jnp.sum(w, axis=0, keepdims=True)

    def scores(g):
        d0[...] = dot(g)
        soft(d0, g)

    def weigh(it, u0, n, at):
        total = jnp.zeros((BLOCK, 128), jnp.float32)
        for j in range(n):
            row = stat_row(u0 + j)
            part = jnp.exp2(ml[pl.ds(row, 1), :] - tot[it, pl.ds(row, 1), :]) / tot[it, pl.ds(row + 4, 1), :]
            w = (p[u0 + j, at, :] * part).astype(jnp.bfloat16)
            wide = w.astype(jnp.float32)
            total += wide[:, :128] + wide[:, 128:]
            wbuf[:, j * UNIT : (j + 1) * UNIT] = w
        block = e[rows(u0 * UNIT, n * UNIT), :]
        return jnp.dot(wbuf[:, : n * UNIT], block, preferred_element_type=jnp.float32), total

    def weigh_half(it, side, h, at):
        add, total = weigh(it, 8 * side + 4 * h, 4, at)
        s[side, at, :] = add if h == 0 else s[side, at, :] + add
        mass[side, at, :] = total if h == 0 else mass[side, at, :] + total

    def weigh_own(it, h):
        @pl.loop(0, K // BLOCK)
        def _(k):
            weigh_half(it, 0, h, rows(k * BLOCK, BLOCK))

    mine, theirs = core * H, (1 - core) * H
    n = H // BLOCK

    def update(it):
        def finish_sums(at):
            for h in range(2):
                weigh_half(it, 1, h, at)
            return s[0, at, :] + s[1, at, :], mass[0, at, :] + mass[1, at, :]

        def give(k):
            at, to = rows(theirs + k * BLOCK, BLOCK), rows(k * BLOCK, BLOCK)
            i = it * n + k
            return (
                remote(s.at[0, at], rs.at[to], rss.at[i], rsr.at[i], twin),
                remote(mass.at[0, at], rsm.at[to], ms.at[i], mr.at[i], twin),
            )

        def spread_new(start, i):
            at = rows(start + i * CHUNK, CHUNK)
            dst = c if it == 0 else out_c
            return remote(c.at[at], dst.at[at], ags.at[it * 4 + i], agr.at[it * 4 + i], twin)

        @pl.loop(0, n)
        def _(k):
            at = rows(theirs + k * BLOCK, BLOCK)
            sums, total = finish_sums(at)
            s[0, at, :] = sums
            mass[0, at, :] = total
            for copy in give(k):
                copy.start()

        @pl.loop(0, n)
        def _(k):
            at, to = rows(mine + k * BLOCK, BLOCK), rows(k * BLOCK, BLOCK)
            sums, total = finish_sums(at)
            for copy in give(k):
                copy.wait_recv()
            total = total + rsm[to, :]
            scale = 1.0 / (jnp.sum(total, axis=1, keepdims=True) + PRIOR)
            for j in range(BLOCK // CHUNK):
                sub = rows(mine + k * BLOCK + j * CHUNK, CHUNK)
                cut = slice(j * CHUNK, (j + 1) * CHUNK)
                add = rs[rows(k * BLOCK + j * CHUNK, CHUNK), :]
                c[sub, :] = (sums[cut, :] + add + PRIOR * c[sub, :]) * scale[cut, :]
                spread_new(mine, 2 * k + j).start()
                if it == 0:
                    prepare(sub)
            if it == 1:
                pltpu.make_async_copy(c.at[at], out_c.at[at], osem.at[k]).start()

        @pl.loop(0, n)
        def _(k):
            for copy in give(k):
                copy.wait_send()
            for j in range(BLOCK // CHUNK):
                spread_new(theirs, 2 * k + j).wait()
                if it == 0:
                    prepare(rows(theirs + k * BLOCK + j * CHUNK, CHUNK))
            if it == 1:
                at = rows(mine + k * BLOCK, BLOCK)
                pltpu.make_async_copy(c.at[at], out_c.at[at], osem.at[k]).wait()

    def pipelined(pairs, hook):
        d0[...] = dot(0)

        @pl.loop(0, pairs)
        def _(k):
            d1[...] = dot(2 * k + 1)
            soft(d0, 2 * k)

            @pl.when(k < pairs - 1)
            def _():
                d0[...] = dot(2 * k + 2)
                soft(d1, 2 * k + 1)

            @pl.when(k == pairs - 1)
            def _():
                soft(d1, 2 * pairs - 1)

            hook(k)

    @pl.loop(0, K // CHUNK)
    def _(k):
        prepare(rows(k * CHUNK, CHUNK))

    told(0)
    tell(1)

    def meanwhile(k):
        @pl.when(k == 0)
        def _():
            told(1)
            tell(2)

        @pl.when(k == 1)
        def _():
            told(2)
            for h in range(2):
                stats_first(0, h)

        forward(k)
        spread(k + 2)

    pipelined(2, meanwhile)
    forward(2)

    @pl.loop(4, 6)
    def _(t):
        spread(t)

    for h in range(2):
        stats_second(0, h)
    forward(3)
    spread(6)

    @pl.loop(4, 8)
    def _(g):
        arrive(2 * g - 8)
        arrive(2 * g - 7)
        scores(g)

        @pl.when(g == 4)
        def _():
            forward(4)
            spread_whole()

            @pl.loop(5, 7)
            def _(t):
                forward(t)

            for h in range(2):
                stats_last(0, h)
                weigh_own(0, h)

    for h in range(2):
        share(0, h).wait_recv()
    update(0)

    def between(k):
        for h in range(2):

            @pl.when(k == h)
            def _():
                stats_first(1, h)

        @pl.when(k == 2)
        def _():
            stats_second(1, 0)

    pipelined(4, between)
    stats_second(1, 1)
    for h in range(2):
        stats_last(1, h)
        weigh_own(1, h)
    for h in range(2):
        share(1, h).wait_recv()
    update(1)

    @pl.loop(0, 56)
    def _(k):
        ref = land.at[pl.ds(0, PIECE)]
        remote(ref, ref, gsend.at[k], grecv.at[0], twin).wait_send()

    for half in range(2):
        ref = land.at[pl.ds(0, 128)]
        remote(ref, ref, gsend.at[56 + half], grecv.at[0], twin).wait_send()

    for it in range(ITERS):
        for h in range(2):
            ref = z1.at[0, 0, 0]
            for k in range(7):
                remote(ref, ref, s1s.at[(it * 2 + h) * 8 + k], s1r.at[0], twin).wait_send()
                remote(ref, ref, s2s.at[(it * 2 + h) * 8 + k], s2r.at[0], twin).wait_send()
            share(it, h).wait_send()

    out_t[...] = tot[1, 0:16, :]


def finish(c, tot, out_c, out_l, hold, reads, writes):
    blocks = [pl.ds(k * CHUNK, CHUNK) for k in range(K // CHUNK)]
    ins = [pltpu.make_async_copy(c.at[at], hold.at[at], reads.at[k]) for k, at in enumerate(blocks)]
    outs = [pltpu.make_async_copy(hold.at[at], out_c.at[at], writes.at[k]) for k, at in enumerate(blocks)]
    for copy in ins:
        copy.start()
    for h in range(2):
        value = (tot[h * 8 : h * 8 + 4, :] + jnp.log2(tot[h * 8 + 4 : h * 8 + 8, :])) * LN2
        for j in range(4):
            at = 8 * h + 2 * j
            out_l[at : at + 1, :] = value[j : j + 1, :128]
            out_l[at + 1 : at + 2, :] = value[j : j + 1, 128:]
    for read, write in zip(ins, outs):
        read.wait()
        write.start()
    for write in outs:
        write.wait()


def local(embeddings, centroids):
    f32, bf16, dma = jnp.float32, jnp.bfloat16, pltpu.SemaphoreType.DMA
    vmem = pltpu.VMEM
    new, stats = pl.pallas_call(
        kernel,
        out_shape=(jax.ShapeDtypeStruct((K, D), f32), jax.ShapeDtypeStruct((16, UNIT), f32)),
        in_specs=[pl.BlockSpec(memory_space=pl.ANY)] * 2,
        out_specs=(pl.BlockSpec(memory_space=pl.ANY), pl.BlockSpec(memory_space=pltpu.VMEM)),
        scratch_shapes=[
            vmem((2 * R, D), bf16),
            vmem((R, D), f32),
            vmem((768, D), f32),
            vmem((K, D), f32),
            vmem((K, D), bf16),
            vmem((K, 128), f32),
            vmem((16, K, UNIT), f32),
            vmem((32, UNIT), f32),
            vmem((2, 2, 8, 8, UNIT), f32),
            vmem((2, 2, 8, 8, UNIT), f32),
            vmem((2, 32, UNIT), f32),
            vmem((2, K, D), f32),
            vmem((2, K, 128), f32),
            vmem((H, D), f32),
            vmem((H, 128), f32),
            vmem((BLOCK, 4 * UNIT), bf16),
            vmem((K, 2 * UNIT), f32),
            vmem((K, 2 * UNIT), f32),
            dma, dma, dma((4,)),
            dma((64,)), dma((64,)),
            dma((32,)), dma((32,)), dma((32,)), dma((32,)),
            dma((4,)), dma((4,)),
            dma((4,)), dma((4,)), dma((4,)), dma((4,)), dma((8,)), dma((8,)),
            pltpu.SemaphoreType.REGULAR((3,)),
        ],
        compiler_params=pltpu.CompilerParams(
            collective_id=0, has_side_effects=True, vmem_limit_bytes=54 << 20
        ),
    )(embeddings, centroids)
    new, logs = pl.pallas_call(
        finish,
        out_shape=(jax.ShapeDtypeStruct((K, D), f32), jax.ShapeDtypeStruct((16, 128), f32)),
        in_specs=[pl.BlockSpec(memory_space=pl.ANY), pl.BlockSpec(memory_space=vmem)],
        out_specs=(pl.BlockSpec(memory_space=pl.ANY), pl.BlockSpec(memory_space=vmem)),
        scratch_shapes=[vmem((K, D), f32), dma((8,)), dma((8,))],
        compiler_params=pltpu.CompilerParams(vmem_limit_bytes=60 << 20),
    )(new, stats)
    return new, logs.reshape(R)


def solution(mesh):
    placed = (P("dp", None), P("cent", None))
    return jax.shard_map(
        local, mesh=mesh, in_specs=placed, out_specs=(P("cent", None), P("dp")), check_vma=False
    )
```

```python
import jax
import jax.numpy as jnp
from jax import lax
from jax.experimental import pallas as pl
from jax.experimental.pallas import tpu as pltpu
from jax.sharding import PartitionSpec as P

MESH = pl.DeviceIdType.MESH
ITERS = 2
LOG2E = 1.4426950408889634
LN2 = 0.6931471805599453
SCALE = 20.0 * LOG2E
PRIOR = 0.5
D = 768
K = 1024
H = 512
R = 2048
UNIT = 256
PIECE = 32
CHUNK = 128
BLOCK = 256
NT = (((1,), (1,)), ((), ()))


def place(x, y, z, core):
    x, y, z = lax.rem(x, 4), lax.rem(y, 4), lax.rem(z, 8)
    return (lax.rem(x, 2) * 2 + core, (z * 4 + y) * 2 + x // 2)


def kernel(
    e_hbm, c_hbm, c, out_l,
    e, land, sb, cb, nrm, p, ml, z1, z2, tot, s, mass, rs, rsm, wbuf, d0, d1,
    esem, csem, gsend, grecv, s1s, s1r, s2s, s2r, fs, fr, rss, rsr, ms, mr, ags, agr, relay,
):
    dp, ct = lax.axis_index("dp"), lax.axis_index("cent")
    core, xlo = lax.rem(dp, 2), dp // 2
    xhi, y, z = lax.rem(ct, 2), lax.rem(ct // 2, 4), ct // 8
    x = xhi * 2 + xlo
    f1 = lax.rem(y + 2 * z, 4)
    f2 = lax.rem(z + 2 * y, 4)

    twin = place(x, y, z, 1 - core)
    xp, xm = place(x + 1, y, z, core), place(x + 3, y, z, core)
    yp, ym = place(x, y + 1, z, core), place(x, y + 3, z, core)
    zp, zm = place(x, y, z + 1, core), place(x, y, z + 7, core)
    partner = (lax.rem(dp + 2, 4), ct)
    zpeers = [place(x, y, z + k, core) for k in range(1, 8)]
    ypeers = [place(x, y + k, z, core) for k in range(1, 4)]
    ypeers += [place(x + 2, y + k, z, core) for k in range(4)]

    ecopy = pltpu.make_async_copy(e_hbm, e.at[pl.ds(0, R)], esem)
    ecopy.start()
    ccopy = pltpu.make_async_copy(c_hbm, c, csem)
    ccopy.start()

    barrier = pltpu.get_barrier_semaphore()
    near = [xp, xm, yp, ym, zp, zm]
    for peer in near + [twin]:
        pl.semaphore_signal(barrier, inc=1, device_id=peer, device_id_type=MESH)

    def rows(start, size):
        return pl.ds(pl.multiple_of(start, size), size)

    def remote(src, dst, ssem, rsem, to):
        return pltpu.make_async_remote_copy(
            src_ref=src, dst_ref=dst, send_sem=ssem, recv_sem=rsem, device_id=to, device_id_type=MESH
        )

    def unit_of(t):
        return jnp.where(t < 6, t, 7)

    def piece(u, half, q):
        return rows(u * UNIT + half * 128 + q * PIECE, PIECE)

    ecopy.wait()
    pl.semaphore_wait(barrier, 7)

    def tell(r):
        for peer in near:
            pl.semaphore_signal(relay.at[r], inc=1, device_id=peer, device_id_type=MESH)

    def told(r):
        pl.semaphore_wait(relay.at[r], 6)

    def spread(t):
        u = unit_of(t)
        for half, q, to in ((0, f1, xm), (1, f2, xp)):
            src = sb.at[rows(t * 64 + half * 32, 32)]
            src[...] = e[piece(u, half, q), :].astype(jnp.float32)
            remote(
                src, land.at[piece(u, half, q)],
                gsend.at[42 + 2 * t + half], grecv.at[u * 8 + half * 4 + q], to,
            ).start()

        @pl.when(t == 6)
        def _():
            for half, q, to in ((0, f1 + 2, xm), (1, f2 + 2, xp)):
                q = lax.rem(q, 4)
                src = sb.at[rows(704 + half * 32, 32)]
                src[...] = e[piece(7, half, q), :].astype(jnp.float32)
                remote(
                    src, land.at[piece(7, half, q)], gsend.at[40 + half], grecv.at[56 + half * 4 + q], to
                ).start()

    def spread_whole():
        for half, to in ((0, xm), (1, xp)):
            src = sb.at[pl.ds(448 + half * 128, 128)]
            src[...] = e[pl.ds(6 * UNIT + half * 128, 128), :].astype(jnp.float32)
            remote(
                src, land.at[pl.ds(6 * UNIT + half * 128, 128)],
                gsend.at[56 + half], grecv.at[48 + half], to,
            ).start()

    spread(0)
    tell(0)

    spread(1)

    def got(u, half, q):
        remote(
            land.at[piece(u, half, q)], land.at[piece(u, half, q)],
            gsend.at[0], grecv.at[u * 8 + half * 4 + q], twin,
        ).wait_recv()

    def forward(t):
        u = unit_of(t)
        odd = lax.rem(t, 2)
        got(u, 0, f1)
        got(u, 1, f2)
        zone = tuple(jnp.where(odd == 0, a, b) for a, b in zip(zp, zm))
        yone = tuple(jnp.where(odd == 0, a, b) for a, b in zip(yp, ym))
        sends = ((0, f1, yp), (1, f2, zp), (0, f1, ym), (1, f2, zm), (0, f1, zone), (1, f2, yone))

        def send(j):
            half, q, to = sends[j]
            ref = land.at[piece(u, half, q)]
            remote(ref, ref, gsend.at[t * 6 + j], grecv.at[u * 8 + half * 4 + q], to).start()

        for j in range(4):
            send(j)

        @pl.when(t < 6)
        def _():
            send(4)
            send(5)


    def arrive(u):
        @pl.when(u == 6)
        def _():
            for half in range(2):
                ref = land.at[pl.ds(6 * UNIT + half * 128, 128)]
                remote(ref, ref, gsend.at[0], grecv.at[48 + half], twin).wait_recv()

        @pl.when(u != 6)
        def _():
            for k in range(1, 4):
                got(u, 0, lax.rem(f1 + k, 4))
                got(u, 1, lax.rem(f2 + k, 4))

        e[rows(R + u * UNIT, UNIT), :] = land[rows(u * UNIT, UNIT), :].astype(jnp.bfloat16)

    ccopy.wait()

    def prepare(at):
        block = c[at, :]
        cb[at, :] = block.astype(jnp.bfloat16)
        nrm[at, :] = jnp.broadcast_to(0.5 * jnp.sum(block * block, axis=1, keepdims=True), (CHUNK, 128))

    def merge(ref, it, h):
        top = ref[it, h, 0, 0:4, :]
        for k in range(1, 8):
            top = jnp.maximum(top, ref[it, h, k, 0:4, :])
        total = jnp.zeros_like(top)
        for k in range(8):
            total += ref[it, h, k, 4:8, :] * jnp.exp2(ref[it, h, k, 0:4, :] - top)
        return top, total

    def send_all(ref, it, h, slot, ssem, rsem, peers):
        for k, to in enumerate(peers):
            at = (it * 2 + h) * 8
            remote(ref.at[it, h, slot], ref.at[it, h, slot], ssem.at[at + k], rsem.at[at + slot], to).start()

    def receive_all(ref, it, h, slot, ssem, rsem):
        for k in range(1, 8):
            src = lax.rem(slot + k, 8)
            at = (it * 2 + h) * 8 + src
            remote(ref.at[it, h, src], ref.at[it, h, src], ssem.at[0], rsem.at[at], twin).wait_recv()

    def stats_first(it, h):
        z1[it, h, z] = ml[h * 8 : h * 8 + 8, :]
        send_all(z1, it, h, z, s1s, s1r, zpeers)

    yslot = y * 2 + xhi

    def stats_second(it, h):
        receive_all(z1, it, h, z, s1s, s1r)
        top, total = merge(z1, it, h)
        z2[it, h, yslot, 0:4, :] = top
        z2[it, h, yslot, 4:8, :] = total
        send_all(z2, it, h, yslot, s2s, s2r, ypeers)

    def share(it, h):
        src, dst = tot.at[it, pl.ds(h * 8, 8)], tot.at[it, pl.ds(16 + h * 8, 8)]
        return remote(src, dst, fs.at[it * 2 + h], fr.at[it * 2 + h], partner)

    def stats_last(it, h):
        receive_all(z2, it, h, yslot, s2s, s2r)
        top, total = merge(z2, it, h)
        tot[it, h * 8 : h * 8 + 4, :] = top
        tot[it, h * 8 + 4 : h * 8 + 8, :] = total
        share(it, h).start()

    def dot(g):
        return lax.dot_general(cb[...], e[rows(g * 512, 512), :], NT, preferred_element_type=jnp.float32)

    def stat_row(u):
        return (u // 4) * 8 + lax.rem(u, 4)

    def soft(d, g):
        n = nrm[...]
        n = jnp.concatenate([n, n], axis=1)
        for j in range(2):
            u = 2 * g + j
            t = (d[:, j * UNIT : (j + 1) * UNIT] - n) * SCALE
            m = jnp.max(t, axis=0, keepdims=True)
            w = jnp.exp2(t - m)
            p[u] = w
            ml[pl.ds(stat_row(u), 1), :] = m
            ml[pl.ds(stat_row(u) + 4, 1), :] = jnp.sum(w, axis=0, keepdims=True)

    def scores(g):
        d0[...] = dot(g)
        soft(d0, g)

    def weigh(it, u0, n, at, slot):
        total = jnp.zeros((BLOCK, 128), jnp.float32)
        for j in range(n):
            row = stat_row(u0 + j)
            part = jnp.exp2(ml[pl.ds(row, 1), :] - tot[it, pl.ds(row, 1), :]) / tot[it, pl.ds(row + 4, 1), :]
            w = (p[u0 + j, at, :] * part).astype(jnp.bfloat16)
            wide = w.astype(jnp.float32)
            total += wide[:, :128] + wide[:, 128:]
            wbuf[slot, :, j * UNIT : (j + 1) * UNIT] = w
        block = e[rows(u0 * UNIT, n * UNIT), :]
        return jnp.dot(wbuf[slot], block, preferred_element_type=jnp.float32), total

    def weigh_half(it, side, h, at, slot):
        add, total = weigh(it, 8 * side + 4 * h, 4, at, slot)
        s[side, at, :] = add if h == 0 else s[side, at, :] + add
        mass[side, at, :] = total if h == 0 else mass[side, at, :] + total

    def weigh_own(it, h):
        @pl.loop(0, K // BLOCK // 2)
        def _(k):
            for j in range(2):
                weigh_half(it, 0, h, rows((2 * k + j) * BLOCK, BLOCK), j)

    mine, theirs = core * H, (1 - core) * H
    n = H // BLOCK

    def update(it):
        def finish_sums(at):
            for h in range(2):
                weigh_half(it, 1, h, at, h)
            return s[0, at, :] + s[1, at, :], mass[0, at, :] + mass[1, at, :]

        def give(k):
            at, to = rows(theirs + k * BLOCK, BLOCK), rows(k * BLOCK, BLOCK)
            i = it * n + k
            return (
                remote(s.at[0, at], rs.at[to], rss.at[i], rsr.at[i], twin),
                remote(mass.at[0, at], rsm.at[to], ms.at[i], mr.at[i], twin),
            )

        def spread_new(start, i):
            at = rows(start + i * CHUNK, CHUNK)
            return remote(c.at[at], c.at[at], ags.at[it * 4 + i], agr.at[it * 4 + i], twin)

        @pl.loop(0, n)
        def _(k):
            at = rows(theirs + k * BLOCK, BLOCK)
            sums, total = finish_sums(at)
            s[0, at, :] = sums
            mass[0, at, :] = total
            for copy in give(k):
                copy.start()

        @pl.loop(0, n)
        def _(k):
            at, to = rows(mine + k * BLOCK, BLOCK), rows(k * BLOCK, BLOCK)
            sums, total = finish_sums(at)
            for copy in give(k):
                copy.wait_recv()
            total = total + rsm[to, :]
            scale = 1.0 / (jnp.sum(total, axis=1, keepdims=True) + PRIOR)
            for j in range(BLOCK // CHUNK):
                sub = rows(mine + k * BLOCK + j * CHUNK, CHUNK)
                cut = slice(j * CHUNK, (j + 1) * CHUNK)
                add = rs[rows(k * BLOCK + j * CHUNK, CHUNK), :]
                c[sub, :] = (sums[cut, :] + add + PRIOR * c[sub, :]) * scale[cut, :]
                spread_new(mine, 2 * k + j).start()
                if it == 0:
                    prepare(sub)

        @pl.loop(0, n)
        def _(k):
            for copy in give(k):
                copy.wait_send()
            for j in range(BLOCK // CHUNK):
                spread_new(theirs, 2 * k + j).wait()
                if it == 0:
                    prepare(rows(theirs + k * BLOCK + j * CHUNK, CHUNK))

    def pipelined(pairs, hook):
        d0[...] = dot(0)

        @pl.loop(0, pairs)
        def _(k):
            d1[...] = dot(2 * k + 1)
            soft(d0, 2 * k)

            @pl.when(k < pairs - 1)
            def _():
                d0[...] = dot(2 * k + 2)
                soft(d1, 2 * k + 1)

            @pl.when(k == pairs - 1)
            def _():
                soft(d1, 2 * pairs - 1)

            hook(k)

    @pl.loop(0, K // CHUNK)
    def _(k):
        prepare(rows(k * CHUNK, CHUNK))

    @pl.loop(2, 7)
    def _(t):
        spread(t)

    told(0)
    tell(1)

    def meanwhile(k):
        @pl.when(k == 0)
        def _():
            told(1)
            tell(2)

        @pl.when(k == 1)
        def _():
            told(2)
            for h in range(2):
                stats_first(0, h)

        forward(k)

    pipelined(2, meanwhile)
    for t in (2, 3):
        forward(t)
    for h in range(2):
        stats_second(0, h)
    spread_whole()
    forward(4)

    @pl.loop(4, 8)
    def _(g):
        arrive(2 * g - 8)
        arrive(2 * g - 7)
        scores(g)

        @pl.when(g == 4)
        def _():
            @pl.loop(5, 7)
            def _(t):
                forward(t)

        @pl.when(g == 5)
        def _():
            for h in range(2):
                stats_last(0, h)
                weigh_own(0, h)

    for h in range(2):
        share(0, h).wait_recv()
    update(0)

    def between(k):
        for h in range(2):

            @pl.when(k == h)
            def _():
                stats_first(1, h)

        @pl.when(k == 2)
        def _():
            stats_second(1, 0)

    pipelined(4, between)
    stats_second(1, 1)
    for h in range(2):
        stats_last(1, h)
        weigh_own(1, h)
    for h in range(2):
        share(1, h).wait_recv()
    update(1)

    @pl.loop(0, 56)
    def _(k):
        ref = land.at[pl.ds(0, PIECE)]
        remote(ref, ref, gsend.at[k], grecv.at[0], twin).wait_send()

    for half in range(2):
        ref = land.at[pl.ds(0, 128)]
        remote(ref, ref, gsend.at[56 + half], grecv.at[0], twin).wait_send()

    for it in range(ITERS):
        for h in range(2):
            ref = z1.at[0, 0, 0]
            for k in range(7):
                remote(ref, ref, s1s.at[(it * 2 + h) * 8 + k], s1r.at[0], twin).wait_send()
                remote(ref, ref, s2s.at[(it * 2 + h) * 8 + k], s2r.at[0], twin).wait_send()
            share(it, h).wait_send()

    for h in range(2):
        value = (tot[1, h * 8 : h * 8 + 4, :] + jnp.log2(tot[1, h * 8 + 4 : h * 8 + 8, :])) * LN2
        for j in range(4):
            at = 8 * h + 2 * j
            out_l[at : at + 1, :] = value[j : j + 1, :128]
            out_l[at + 1 : at + 2, :] = value[j : j + 1, 128:]


def local(embeddings, centroids):
    f32, bf16, dma = jnp.float32, jnp.bfloat16, pltpu.SemaphoreType.DMA
    vmem = pltpu.VMEM
    new, logs = pl.pallas_call(
        kernel,
        out_shape=(vmem((K, D), f32), vmem((16, 128), f32)),
        in_specs=[pl.BlockSpec(memory_space=pl.ANY)] * 2,
        out_specs=(pl.BlockSpec(memory_space=vmem), pl.BlockSpec(memory_space=vmem)),
        scratch_shapes=[
            vmem((2 * R, D), bf16),
            vmem((R, D), f32),
            vmem((768, D), f32),
            vmem((K, D), bf16),
            vmem((K, 128), f32),
            vmem((16, K, UNIT), f32),
            vmem((32, UNIT), f32),
            vmem((2, 2, 8, 8, UNIT), f32),
            vmem((2, 2, 8, 8, UNIT), f32),
            vmem((2, 32, UNIT), f32),
            vmem((2, K, D), f32),
            vmem((2, K, 128), f32),
            vmem((H, D), f32),
            vmem((H, 128), f32),
            vmem((2, BLOCK, 4 * UNIT), bf16),
            vmem((K, 2 * UNIT), f32),
            vmem((K, 2 * UNIT), f32),
            dma, dma,
            dma((64,)), dma((64,)),
            dma((32,)), dma((32,)), dma((32,)), dma((32,)),
            dma((4,)), dma((4,)),
            dma((4,)), dma((4,)), dma((4,)), dma((4,)), dma((8,)), dma((8,)),
            pltpu.SemaphoreType.REGULAR((3,)),
        ],
        compiler_params=pltpu.CompilerParams(
            collective_id=0, has_side_effects=True, vmem_limit_bytes=54 << 20
        ),
    )(embeddings, centroids)
    return new, logs.reshape(R)


def solution(mesh):
    placed = (P("dp", None), P("cent", None))
    return jax.shard_map(
        local, mesh=mesh, in_specs=placed, out_specs=(P("cent", None), P("dp")), check_vma=False
    )
```

```python
import jax
import jax.numpy as jnp
from jax import lax
from jax.experimental import pallas as pl
from jax.experimental.pallas import tpu as pltpu
from jax.sharding import PartitionSpec as P

MESH = pl.DeviceIdType.MESH
ITERS = 2
LOG2E = 1.4426950408889634
LN2 = 0.6931471805599453
SCALE = 20.0 * LOG2E
PRIOR = 0.5
D = 768
K = 1024
H = 512
R = 2048
UNIT = 256
PIECE = 32
CHUNK = 128
BLOCK = 256
NT = (((1,), (1,)), ((), ()))


def place(x, y, z, core):
    x, y, z = lax.rem(x, 4), lax.rem(y, 4), lax.rem(z, 8)
    return (lax.rem(x, 2) * 2 + core, (z * 4 + y) * 2 + x // 2)


def kernel(
    e_hbm, c_hbm, c, out_l,
    e, land, sb, cb, nrm, p, ml, z1, z2, tot, s, mass, rs, rsm, wbuf, d0, d1,
    esem, csem, gsend, grecv, s1s, s1r, s2s, s2r, fs, fr, rss, rsr, ms, mr, ags, agr, relay,
):
    dp, ct = lax.axis_index("dp"), lax.axis_index("cent")
    core, xlo = lax.rem(dp, 2), dp // 2
    xhi, y, z = lax.rem(ct, 2), lax.rem(ct // 2, 4), ct // 8
    x = xhi * 2 + xlo
    f1 = lax.rem(y + 2 * z, 4)
    f2 = lax.rem(z + 2 * y, 4)

    twin = place(x, y, z, 1 - core)
    xp, xm = place(x + 1, y, z, core), place(x + 3, y, z, core)
    yp, ym = place(x, y + 1, z, core), place(x, y + 3, z, core)
    zp, zm = place(x, y, z + 1, core), place(x, y, z + 7, core)
    partner = (lax.rem(dp + 2, 4), ct)
    zpeers = [place(x, y, z + k, core) for k in range(1, 8)]
    ypeers = [place(x, y + k, z, core) for k in range(1, 4)]
    ypeers += [place(x + 2, y + k, z, core) for k in range(4)]

    ecopy = pltpu.make_async_copy(e_hbm, e.at[pl.ds(0, R)], esem)
    ecopy.start()
    ccopy = pltpu.make_async_copy(c_hbm, c, csem)
    ccopy.start()

    barrier = pltpu.get_barrier_semaphore()
    near = [xp, xm, yp, ym, zp, zm]
    for peer in near + [twin]:
        pl.semaphore_signal(barrier, inc=1, device_id=peer, device_id_type=MESH)

    def rows(start, size):
        return pl.ds(pl.multiple_of(start, size), size)

    def remote(src, dst, ssem, rsem, to):
        return pltpu.make_async_remote_copy(
            src_ref=src, dst_ref=dst, send_sem=ssem, recv_sem=rsem, device_id=to, device_id_type=MESH
        )

    def unit_of(t):
        return jnp.where(t < 6, t, 7)

    def piece(u, half, q):
        return rows(u * UNIT + half * 128 + q * PIECE, PIECE)

    ecopy.wait()
    pl.semaphore_wait(barrier, 7)

    def tell(r):
        for peer in near:
            pl.semaphore_signal(relay.at[r], inc=1, device_id=peer, device_id_type=MESH)

    def told(r):
        pl.semaphore_wait(relay.at[r], 6)

    def spread(t):
        u = unit_of(t)
        for half, q, to in ((0, f1, xm), (1, f2, xp)):
            src = sb.at[rows(t * 64 + half * 32, 32)]
            src[...] = e[piece(u, half, q), :].astype(jnp.float32)
            remote(
                src, land.at[piece(u, half, q)],
                gsend.at[42 + 2 * t + half], grecv.at[u * 8 + half * 4 + q], to,
            ).start()

        @pl.when(t == 6)
        def _():
            for half, q, to in ((0, f1 + 2, xm), (1, f2 + 2, xp)):
                q = lax.rem(q, 4)
                src = sb.at[rows(704 + half * 32, 32)]
                src[...] = e[piece(7, half, q), :].astype(jnp.float32)
                remote(
                    src, land.at[piece(7, half, q)], gsend.at[40 + half], grecv.at[56 + half * 4 + q], to
                ).start()

    def spread_whole():
        for half, to in ((0, xm), (1, xp)):
            src = sb.at[pl.ds(448 + half * 128, 128)]
            src[...] = e[pl.ds(6 * UNIT + half * 128, 128), :].astype(jnp.float32)
            remote(
                src, land.at[pl.ds(6 * UNIT + half * 128, 128)],
                gsend.at[56 + half], grecv.at[48 + half], to,
            ).start()

    spread(0)
    tell(0)

    spread(1)

    def got(u, half, q):
        remote(
            land.at[piece(u, half, q)], land.at[piece(u, half, q)],
            gsend.at[0], grecv.at[u * 8 + half * 4 + q], twin,
        ).wait_recv()

    def forward(t):
        u = unit_of(t)
        odd = lax.rem(t, 2)
        got(u, 0, f1)
        got(u, 1, f2)
        zone = tuple(jnp.where(odd == 0, a, b) for a, b in zip(zp, zm))
        yone = tuple(jnp.where(odd == 0, a, b) for a, b in zip(yp, ym))
        sends = ((0, f1, yp), (1, f2, zp), (0, f1, ym), (1, f2, zm), (0, f1, zone), (1, f2, yone))

        def send(j):
            half, q, to = sends[j]
            ref = land.at[piece(u, half, q)]
            remote(ref, ref, gsend.at[t * 6 + j], grecv.at[u * 8 + half * 4 + q], to).start()

        for j in range(4):
            send(j)

        @pl.when(t < 6)
        def _():
            send(4)
            send(5)


    def arrive(u):
        @pl.when(u == 6)
        def _():
            for half in range(2):
                ref = land.at[pl.ds(6 * UNIT + half * 128, 128)]
                remote(ref, ref, gsend.at[0], grecv.at[48 + half], twin).wait_recv()

        @pl.when(u != 6)
        def _():
            for k in range(1, 4):
                got(u, 0, lax.rem(f1 + k, 4))
                got(u, 1, lax.rem(f2 + k, 4))

        e[rows(R + u * UNIT, UNIT), :] = land[rows(u * UNIT, UNIT), :].astype(jnp.bfloat16)

    ccopy.wait()

    def prepare(at):
        block = c[at, :]
        cb[at, :] = block.astype(jnp.bfloat16)
        nrm[at, :] = jnp.broadcast_to(0.5 * jnp.sum(block * block, axis=1, keepdims=True), (CHUNK, 128))

    def merge(ref, it, h):
        top = ref[it, h, 0, 0:4, :]
        for k in range(1, 8):
            top = jnp.maximum(top, ref[it, h, k, 0:4, :])
        total = jnp.zeros_like(top)
        for k in range(8):
            total += ref[it, h, k, 4:8, :] * jnp.exp2(ref[it, h, k, 0:4, :] - top)
        return top, total

    def send_all(ref, it, h, slot, ssem, rsem, peers):
        for k, to in enumerate(peers):
            at = (it * 2 + h) * 8
            remote(ref.at[it, h, slot], ref.at[it, h, slot], ssem.at[at + k], rsem.at[at + slot], to).start()

    def receive_all(ref, it, h, slot, ssem, rsem):
        for k in range(1, 8):
            src = lax.rem(slot + k, 8)
            at = (it * 2 + h) * 8 + src
            remote(ref.at[it, h, src], ref.at[it, h, src], ssem.at[0], rsem.at[at], twin).wait_recv()

    def stats_first(it, h):
        z1[it, h, z] = ml[h * 8 : h * 8 + 8, :]
        send_all(z1, it, h, z, s1s, s1r, zpeers)

    yslot = y * 2 + xhi

    def stats_second(it, h):
        receive_all(z1, it, h, z, s1s, s1r)
        top, total = merge(z1, it, h)
        z2[it, h, yslot, 0:4, :] = top
        z2[it, h, yslot, 4:8, :] = total
        send_all(z2, it, h, yslot, s2s, s2r, ypeers)

    def share(it, h):
        src, dst = tot.at[it, pl.ds(h * 8, 8)], tot.at[it, pl.ds(16 + h * 8, 8)]
        return remote(src, dst, fs.at[it * 2 + h], fr.at[it * 2 + h], partner)

    def stats_last(it, h):
        receive_all(z2, it, h, yslot, s2s, s2r)
        top, total = merge(z2, it, h)
        tot[it, h * 8 : h * 8 + 4, :] = top
        tot[it, h * 8 + 4 : h * 8 + 8, :] = total
        share(it, h).start()

    def dot(g):
        return lax.dot_general(cb[...], e[rows(g * 512, 512), :], NT, preferred_element_type=jnp.float32)

    def dot_first(start):
        at = rows(start, H)
        d0[at, :] = lax.dot_general(cb[at, :], e[pl.ds(0, 512), :], NT, preferred_element_type=jnp.float32)

    def stat_row(u):
        return (u // 4) * 8 + lax.rem(u, 4)

    def soft(d, g):
        n = nrm[...]
        n = jnp.concatenate([n, n], axis=1)
        for j in range(2):
            u = 2 * g + j
            t = (d[:, j * UNIT : (j + 1) * UNIT] - n) * SCALE
            m = jnp.max(t, axis=0, keepdims=True)
            w = jnp.exp2(t - m)
            p[u] = w
            ml[pl.ds(stat_row(u), 1), :] = m
            ml[pl.ds(stat_row(u) + 4, 1), :] = jnp.sum(w, axis=0, keepdims=True)

    def scores(g):
        d0[...] = dot(g)
        soft(d0, g)

    def weigh(it, u0, n, at, slot):
        total = jnp.zeros((BLOCK, 128), jnp.float32)
        for j in range(n):
            row = stat_row(u0 + j)
            part = jnp.exp2(ml[pl.ds(row, 1), :] - tot[it, pl.ds(row, 1), :]) / tot[it, pl.ds(row + 4, 1), :]
            w = (p[u0 + j, at, :] * part).astype(jnp.bfloat16)
            wide = w.astype(jnp.float32)
            total += wide[:, :128] + wide[:, 128:]
            wbuf[slot, :, j * UNIT : (j + 1) * UNIT] = w
        block = e[rows(u0 * UNIT, n * UNIT), :]
        return jnp.dot(wbuf[slot], block, preferred_element_type=jnp.float32), total

    def weigh_half(it, side, h, at, slot):
        add, total = weigh(it, 8 * side + 4 * h, 4, at, slot)
        s[side, at, :] = add if h == 0 else s[side, at, :] + add
        mass[side, at, :] = total if h == 0 else mass[side, at, :] + total

    def weigh_own(it, h):
        @pl.loop(0, K // BLOCK // 2)
        def _(k):
            for j in range(2):
                weigh_half(it, 0, h, rows((2 * k + j) * BLOCK, BLOCK), j)

    mine, theirs = core * H, (1 - core) * H
    n = H // BLOCK

    def update(it):
        def finish_sums(at):
            for h in range(2):
                weigh_half(it, 1, h, at, h)
            return s[0, at, :] + s[1, at, :], mass[0, at, :] + mass[1, at, :]

        def give(k):
            at, to = rows(theirs + k * BLOCK, BLOCK), rows(k * BLOCK, BLOCK)
            i = it * n + k
            return (
                remote(s.at[0, at], rs.at[to], rss.at[i], rsr.at[i], twin),
                remote(mass.at[0, at], rsm.at[to], ms.at[i], mr.at[i], twin),
            )

        def spread_new(start, i):
            at = rows(start + i * CHUNK, CHUNK)
            return remote(c.at[at], c.at[at], ags.at[it * 4 + i], agr.at[it * 4 + i], twin)

        @pl.loop(0, n)
        def _(k):
            at = rows(theirs + k * BLOCK, BLOCK)
            sums, total = finish_sums(at)
            s[0, at, :] = sums
            mass[0, at, :] = total
            for copy in give(k):
                copy.start()

        @pl.loop(0, n)
        def _(k):
            at, to = rows(mine + k * BLOCK, BLOCK), rows(k * BLOCK, BLOCK)
            sums, total = finish_sums(at)
            for copy in give(k):
                copy.wait_recv()
            total = total + rsm[to, :]
            scale = 1.0 / (jnp.sum(total, axis=1, keepdims=True) + PRIOR)
            for j in range(BLOCK // CHUNK):
                sub = rows(mine + k * BLOCK + j * CHUNK, CHUNK)
                cut = slice(j * CHUNK, (j + 1) * CHUNK)
                add = rs[rows(k * BLOCK + j * CHUNK, CHUNK), :]
                c[sub, :] = (sums[cut, :] + add + PRIOR * c[sub, :]) * scale[cut, :]
                spread_new(mine, 2 * k + j).start()
                if it == 0:
                    prepare(sub)

        if it == 0:
            dot_first(mine)

        @pl.loop(0, n)
        def _(k):
            for copy in give(k):
                copy.wait_send()
            for j in range(BLOCK // CHUNK):
                spread_new(theirs, 2 * k + j).wait()
                if it == 0:
                    prepare(rows(theirs + k * BLOCK + j * CHUNK, CHUNK))

        if it == 0:
            dot_first(theirs)

    def pipelined(pairs, mid, hook, ready):
        if not ready:
            d0[...] = dot(0)

        @pl.loop(0, pairs)
        def _(k):
            d1[...] = dot(2 * k + 1)
            soft(d0, 2 * k)
            mid(k)

            @pl.when(k < pairs - 1)
            def _():
                d0[...] = dot(2 * k + 2)
                soft(d1, 2 * k + 1)

            @pl.when(k == pairs - 1)
            def _():
                soft(d1, 2 * pairs - 1)

            hook(k)

    @pl.loop(0, K // CHUNK)
    def _(k):
        prepare(rows(k * CHUNK, CHUNK))

    @pl.loop(2, 7)
    def _(t):
        spread(t)

    told(0)
    tell(1)

    def meanwhile(k):
        forward(k)

        @pl.when(k == 0)
        def _():
            told(1)
            tell(2)

        @pl.when(k == 1)
        def _():
            told(2)

    pipelined(2, meanwhile, lambda k: None, False)
    for h in range(2):
        stats_first(0, h)
    for t in (2, 3):
        forward(t)
    for h in range(2):
        stats_second(0, h)
    spread_whole()
    forward(4)

    @pl.loop(4, 8)
    def _(g):
        arrive(2 * g - 8)
        arrive(2 * g - 7)
        scores(g)

        @pl.when(g == 4)
        def _():
            @pl.loop(5, 7)
            def _(t):
                forward(t)

        @pl.when(g == 5)
        def _():
            for h in range(2):
                stats_last(0, h)
                weigh_own(0, h)

    for h in range(2):
        share(0, h).wait_recv()
    update(0)

    def between(k):
        for h in range(2):

            @pl.when(k == h)
            def _():
                stats_first(1, h)

        @pl.when(k == 2)
        def _():
            stats_second(1, 0)

    pipelined(4, lambda k: None, between, True)
    stats_second(1, 1)
    for h in range(2):
        stats_last(1, h)
        weigh_own(1, h)
    for h in range(2):
        share(1, h).wait_recv()
    update(1)

    @pl.loop(0, 56)
    def _(k):
        ref = land.at[pl.ds(0, PIECE)]
        remote(ref, ref, gsend.at[k], grecv.at[0], twin).wait_send()

    for half in range(2):
        ref = land.at[pl.ds(0, 128)]
        remote(ref, ref, gsend.at[56 + half], grecv.at[0], twin).wait_send()

    for it in range(ITERS):
        for h in range(2):
            ref = z1.at[0, 0, 0]
            for k in range(7):
                remote(ref, ref, s1s.at[(it * 2 + h) * 8 + k], s1r.at[0], twin).wait_send()
                remote(ref, ref, s2s.at[(it * 2 + h) * 8 + k], s2r.at[0], twin).wait_send()
            share(it, h).wait_send()

    for h in range(2):
        value = (tot[1, h * 8 : h * 8 + 4, :] + jnp.log2(tot[1, h * 8 + 4 : h * 8 + 8, :])) * LN2
        for j in range(4):
            at = 8 * h + 2 * j
            out_l[at : at + 1, :] = value[j : j + 1, :128]
            out_l[at + 1 : at + 2, :] = value[j : j + 1, 128:]


def local(embeddings, centroids):
    f32, bf16, dma = jnp.float32, jnp.bfloat16, pltpu.SemaphoreType.DMA
    vmem = pltpu.VMEM
    new, logs = pl.pallas_call(
        kernel,
        out_shape=(vmem((K, D), f32), vmem((16, 128), f32)),
        in_specs=[pl.BlockSpec(memory_space=pl.ANY)] * 2,
        out_specs=(pl.BlockSpec(memory_space=vmem), pl.BlockSpec(memory_space=vmem)),
        scratch_shapes=[
            vmem((2 * R, D), bf16),
            vmem((R, D), f32),
            vmem((768, D), f32),
            vmem((K, D), bf16),
            vmem((K, 128), f32),
            vmem((16, K, UNIT), f32),
            vmem((32, UNIT), f32),
            vmem((2, 2, 8, 8, UNIT), f32),
            vmem((2, 2, 8, 8, UNIT), f32),
            vmem((2, 32, UNIT), f32),
            vmem((2, K, D), f32),
            vmem((2, K, 128), f32),
            vmem((H, D), f32),
            vmem((H, 128), f32),
            vmem((2, BLOCK, 4 * UNIT), bf16),
            vmem((K, 2 * UNIT), f32),
            vmem((K, 2 * UNIT), f32),
            dma, dma,
            dma((64,)), dma((64,)),
            dma((32,)), dma((32,)), dma((32,)), dma((32,)),
            dma((4,)), dma((4,)),
            dma((4,)), dma((4,)), dma((4,)), dma((4,)), dma((8,)), dma((8,)),
            pltpu.SemaphoreType.REGULAR((3,)),
        ],
        compiler_params=pltpu.CompilerParams(
            collective_id=0, has_side_effects=True, vmem_limit_bytes=54 << 20
        ),
    )(embeddings, centroids)
    return new, logs.reshape(R)


def solution(mesh):
    placed = (P("dp", None), P("cent", None))
    return jax.shard_map(
        local, mesh=mesh, in_specs=placed, out_specs=(P("cent", None), P("dp")), check_vma=False
    )
```

```python
import jax
import jax.numpy as jnp
from jax import lax
from jax.experimental import pallas as pl
from jax.experimental.pallas import tpu as pltpu
from jax.sharding import PartitionSpec as P

MESH = pl.DeviceIdType.MESH
ITERS = 2
LOG2E = 1.4426950408889634
LN2 = 0.6931471805599453
SCALE = 20.0 * LOG2E
PRIOR = 0.5
D = 768
K = 1024
H = 512
R = 2048
UNIT = 256
PIECE = 32
CHUNK = 128
BLOCK = 256
NT = (((1,), (1,)), ((), ()))


def place(x, y, z, core):
    x, y, z = lax.rem(x, 4), lax.rem(y, 4), lax.rem(z, 8)
    return (lax.rem(x, 2) * 2 + core, (z * 4 + y) * 2 + x // 2)


def kernel(
    e_hbm, c_hbm, c, out_l,
    e, land, sb, cb, nrm, p, ml, z1, z2, tot, s, mass, rs, rsm, wbuf, d0, d1,
    esem, csem, gsend, grecv, s1s, s1r, s2s, s2r, fs, fr, rss, rsr, ms, mr, ags, agr, relay,
):
    dp, ct = lax.axis_index("dp"), lax.axis_index("cent")
    core, xlo = lax.rem(dp, 2), dp // 2
    xhi, y, z = lax.rem(ct, 2), lax.rem(ct // 2, 4), ct // 8
    x = xhi * 2 + xlo
    f1 = lax.rem(y + 2 * z, 4)
    f2 = lax.rem(z + 2 * y, 4)

    twin = place(x, y, z, 1 - core)
    xp, xm = place(x + 1, y, z, core), place(x + 3, y, z, core)
    yp, ym = place(x, y + 1, z, core), place(x, y + 3, z, core)
    zp, zm = place(x, y, z + 1, core), place(x, y, z + 7, core)
    partner = (lax.rem(dp + 2, 4), ct)
    zpeers = [place(x, y, z + k, core) for k in range(1, 8)]
    ypeers = [place(x, y + k, z, core) for k in range(1, 4)]
    ypeers += [place(x + 2, y + k, z, core) for k in range(4)]

    ecopy = pltpu.make_async_copy(e_hbm, e.at[pl.ds(0, R)], esem)
    ecopy.start()
    ccopy = pltpu.make_async_copy(c_hbm, c, csem)
    ccopy.start()

    barrier = pltpu.get_barrier_semaphore()
    near = [xp, xm, yp, ym, zp, zm]
    for peer in near + [twin]:
        pl.semaphore_signal(barrier, inc=1, device_id=peer, device_id_type=MESH)

    def rows(start, size):
        return pl.ds(pl.multiple_of(start, size), size)

    def remote(src, dst, ssem, rsem, to):
        return pltpu.make_async_remote_copy(
            src_ref=src, dst_ref=dst, send_sem=ssem, recv_sem=rsem, device_id=to, device_id_type=MESH
        )

    def unit_of(t):
        return jnp.where(t < 6, t, 7)

    def piece(u, half, q):
        return rows(u * UNIT + half * 128 + q * PIECE, PIECE)

    ecopy.wait()
    pl.semaphore_wait(barrier, 7)

    def tell(r):
        for peer in near:
            pl.semaphore_signal(relay.at[r], inc=1, device_id=peer, device_id_type=MESH)

    def told(r):
        pl.semaphore_wait(relay.at[r], 6)

    def spread(t):
        u = unit_of(t)
        for half, q, to in ((0, f1, xm), (1, f2, xp)):
            src = sb.at[rows(t * 64 + half * 32, 32)]
            src[...] = e[piece(u, half, q), :].astype(jnp.float32)
            remote(
                src, land.at[piece(u, half, q)],
                gsend.at[42 + 2 * t + half], grecv.at[u * 8 + half * 4 + q], to,
            ).start()

        @pl.when(t == 6)
        def _():
            for half, q, to in ((0, f1 + 2, xm), (1, f2 + 2, xp)):
                q = lax.rem(q, 4)
                src = sb.at[rows(704 + half * 32, 32)]
                src[...] = e[piece(7, half, q), :].astype(jnp.float32)
                remote(
                    src, land.at[piece(7, half, q)], gsend.at[40 + half], grecv.at[56 + half * 4 + q], to
                ).start()

    def spread_whole():
        for half, to in ((0, xm), (1, xp)):
            src = sb.at[pl.ds(448 + half * 128, 128)]
            src[...] = e[pl.ds(6 * UNIT + half * 128, 128), :].astype(jnp.float32)
            remote(
                src, land.at[pl.ds(6 * UNIT + half * 128, 128)],
                gsend.at[56 + half], grecv.at[48 + half], to,
            ).start()

    spread(0)
    tell(0)

    spread(1)

    def got(u, half, q):
        remote(
            land.at[piece(u, half, q)], land.at[piece(u, half, q)],
            gsend.at[0], grecv.at[u * 8 + half * 4 + q], twin,
        ).wait_recv()

    def forward(t):
        u = unit_of(t)
        odd = lax.rem(t, 2)
        got(u, 0, f1)
        got(u, 1, f2)
        zone = tuple(jnp.where(odd == 0, a, b) for a, b in zip(zp, zm))
        yone = tuple(jnp.where(odd == 0, a, b) for a, b in zip(yp, ym))
        sends = ((0, f1, yp), (1, f2, zp), (0, f1, ym), (1, f2, zm), (0, f1, zone), (1, f2, yone))

        def send(j):
            half, q, to = sends[j]
            ref = land.at[piece(u, half, q)]
            remote(ref, ref, gsend.at[t * 6 + j], grecv.at[u * 8 + half * 4 + q], to).start()

        for j in range(4):
            send(j)

        @pl.when(t < 6)
        def _():
            send(4)
            send(5)


    def arrive(u):
        @pl.when(u == 6)
        def _():
            for half in range(2):
                ref = land.at[pl.ds(6 * UNIT + half * 128, 128)]
                remote(ref, ref, gsend.at[0], grecv.at[48 + half], twin).wait_recv()

        @pl.when(u != 6)
        def _():
            for k in range(1, 4):
                got(u, 0, lax.rem(f1 + k, 4))
                got(u, 1, lax.rem(f2 + k, 4))

        e[rows(R + u * UNIT, UNIT), :] = land[rows(u * UNIT, UNIT), :].astype(jnp.bfloat16)

    ccopy.wait()

    def prepare(at):
        block = c[at, :]
        cb[at, :] = block.astype(jnp.bfloat16)
        nrm[at, :] = jnp.broadcast_to(0.5 * jnp.sum(block * block, axis=1, keepdims=True), (CHUNK, 128))

    def merge(ref, it, h):
        top = ref[it, h, 0, 0:4, :]
        for k in range(1, 8):
            top = jnp.maximum(top, ref[it, h, k, 0:4, :])
        total = jnp.zeros_like(top)
        for k in range(8):
            total += ref[it, h, k, 4:8, :] * jnp.exp2(ref[it, h, k, 0:4, :] - top)
        return top, total

    def send_all(ref, it, h, slot, ssem, rsem, peers):
        for k, to in enumerate(peers):
            at = (it * 2 + h) * 8
            remote(ref.at[it, h, slot], ref.at[it, h, slot], ssem.at[at + k], rsem.at[at + slot], to).start()

    def receive_all(ref, it, h, slot, ssem, rsem):
        for k in range(1, 8):
            src = lax.rem(slot + k, 8)
            at = (it * 2 + h) * 8 + src
            remote(ref.at[it, h, src], ref.at[it, h, src], ssem.at[0], rsem.at[at], twin).wait_recv()

    def stats_first(it, h):
        z1[it, h, z] = ml[h * 8 : h * 8 + 8, :]
        send_all(z1, it, h, z, s1s, s1r, zpeers)

    yslot = y * 2 + xhi

    def stats_second(it, h):
        receive_all(z1, it, h, z, s1s, s1r)
        top, total = merge(z1, it, h)
        z2[it, h, yslot, 0:4, :] = top
        z2[it, h, yslot, 4:8, :] = total
        send_all(z2, it, h, yslot, s2s, s2r, ypeers)

    def share(it, h):
        src, dst = tot.at[it, pl.ds(h * 8, 8)], tot.at[it, pl.ds(16 + h * 8, 8)]
        return remote(src, dst, fs.at[it * 2 + h], fr.at[it * 2 + h], partner)

    def stats_last(it, h):
        receive_all(z2, it, h, yslot, s2s, s2r)
        top, total = merge(z2, it, h)
        tot[it, h * 8 : h * 8 + 4, :] = top
        tot[it, h * 8 + 4 : h * 8 + 8, :] = total
        share(it, h).start()

    def dot(g):
        return lax.dot_general(cb[...], e[rows(g * 512, 512), :], NT, preferred_element_type=jnp.float32)

    def dot_first(start, size):
        at = rows(start, size)
        d0[at, :] = lax.dot_general(cb[at, :], e[pl.ds(0, 512), :], NT, preferred_element_type=jnp.float32)

    def stat_row(u):
        return (u // 4) * 8 + lax.rem(u, 4)

    def soft(d, g):
        n = nrm[...]
        n = jnp.concatenate([n, n], axis=1)
        for j in range(2):
            u = 2 * g + j
            t = (d[:, j * UNIT : (j + 1) * UNIT] - n) * SCALE
            m = jnp.max(t, axis=0, keepdims=True)
            w = jnp.exp2(t - m)
            p[u] = w
            ml[pl.ds(stat_row(u), 1), :] = m
            ml[pl.ds(stat_row(u) + 4, 1), :] = jnp.sum(w, axis=0, keepdims=True)

    def scores(g):
        d0[...] = dot(g)
        soft(d0, g)

    def weigh(it, u0, n, at, slot):
        total = jnp.zeros((BLOCK, 128), jnp.float32)
        for j in range(n):
            row = stat_row(u0 + j)
            part = jnp.exp2(ml[pl.ds(row, 1), :] - tot[it, pl.ds(row, 1), :]) / tot[it, pl.ds(row + 4, 1), :]
            w = (p[u0 + j, at, :] * part).astype(jnp.bfloat16)
            wide = w.astype(jnp.float32)
            total += wide[:, :128] + wide[:, 128:]
            wbuf[slot, :, j * UNIT : (j + 1) * UNIT] = w
        block = e[rows(u0 * UNIT, n * UNIT), :]
        return jnp.dot(wbuf[slot], block, preferred_element_type=jnp.float32), total

    def weigh_half(it, side, h, at, slot):
        add, total = weigh(it, 8 * side + 4 * h, 4, at, slot)
        s[side, at, :] = add if h == 0 else s[side, at, :] + add
        mass[side, at, :] = total if h == 0 else mass[side, at, :] + total

    def weigh_own(it, h):
        @pl.loop(0, K // BLOCK // 2)
        def _(k):
            for j in range(2):
                weigh_half(it, 0, h, rows((2 * k + j) * BLOCK, BLOCK), j)

    mine, theirs = core * H, (1 - core) * H
    n = H // BLOCK

    def update(it):
        def finish_sums(at):
            for h in range(2):
                weigh_half(it, 1, h, at, h)
            return s[0, at, :] + s[1, at, :], mass[0, at, :] + mass[1, at, :]

        def give(k):
            at, to = rows(theirs + k * BLOCK, BLOCK), rows(k * BLOCK, BLOCK)
            i = it * n + k
            return (
                remote(s.at[0, at], rs.at[to], rss.at[i], rsr.at[i], twin),
                remote(mass.at[0, at], rsm.at[to], ms.at[i], mr.at[i], twin),
            )

        def spread_new(start, i):
            at = rows(start + i * CHUNK, CHUNK)
            return remote(c.at[at], c.at[at], ags.at[it * 4 + i], agr.at[it * 4 + i], twin)

        @pl.loop(0, n)
        def _(k):
            at = rows(theirs + k * BLOCK, BLOCK)
            sums, total = finish_sums(at)
            s[0, at, :] = sums
            mass[0, at, :] = total
            for copy in give(k):
                copy.start()

        @pl.loop(0, n)
        def _(k):
            at, to = rows(mine + k * BLOCK, BLOCK), rows(k * BLOCK, BLOCK)
            sums, total = finish_sums(at)
            for copy in give(k):
                copy.wait_recv()
            total = total + rsm[to, :]
            scale = 1.0 / (jnp.sum(total, axis=1, keepdims=True) + PRIOR)
            for j in range(BLOCK // CHUNK):
                sub = rows(mine + k * BLOCK + j * CHUNK, CHUNK)
                cut = slice(j * CHUNK, (j + 1) * CHUNK)
                add = rs[rows(k * BLOCK + j * CHUNK, CHUNK), :]
                c[sub, :] = (sums[cut, :] + add + PRIOR * c[sub, :]) * scale[cut, :]
                spread_new(mine, 2 * k + j).start()
                if it == 0:
                    prepare(sub)

        if it == 0:
            dot_first(mine, H)

        @pl.loop(0, n)
        def _(k):
            for copy in give(k):
                copy.wait_send()
            for j in range(BLOCK // CHUNK):
                spread_new(theirs, 2 * k + j).wait()
                if it == 0:
                    prepare(rows(theirs + k * BLOCK + j * CHUNK, CHUNK))
                    if j == 1:
                        dot_first(theirs + k * BLOCK, BLOCK)

    def pipelined(pairs, mid, hook, ready):
        if not ready:
            d0[...] = dot(0)

        @pl.loop(0, pairs)
        def _(k):
            d1[...] = dot(2 * k + 1)
            soft(d0, 2 * k)
            mid(k)

            @pl.when(k < pairs - 1)
            def _():
                d0[...] = dot(2 * k + 2)
                soft(d1, 2 * k + 1)

            @pl.when(k == pairs - 1)
            def _():
                soft(d1, 2 * pairs - 1)

            hook(k)

    @pl.loop(0, K // CHUNK)
    def _(k):
        prepare(rows(k * CHUNK, CHUNK))

    @pl.loop(2, 7)
    def _(t):
        spread(t)

    told(0)
    tell(1)

    def meanwhile(k):
        forward(k)

        @pl.when(k == 0)
        def _():
            told(1)
            tell(2)

        @pl.when(k == 1)
        def _():
            told(2)

    pipelined(2, meanwhile, lambda k: None, False)
    for h in range(2):
        stats_first(0, h)
    for t in (2, 3):
        forward(t)
    for h in range(2):
        stats_second(0, h)
    spread_whole()
    forward(4)

    @pl.loop(4, 8)
    def _(g):
        arrive(2 * g - 8)
        arrive(2 * g - 7)
        scores(g)

        @pl.when(g == 4)
        def _():
            @pl.loop(5, 7)
            def _(t):
                forward(t)

        @pl.when(g == 5)
        def _():
            for h in range(2):
                stats_last(0, h)
                weigh_own(0, h)

    for h in range(2):
        share(0, h).wait_recv()
    update(0)

    def between(k):
        for h in range(2):

            @pl.when(k == h)
            def _():
                stats_first(1, h)

        @pl.when(k == 2)
        def _():
            stats_second(1, 0)

    pipelined(4, lambda k: None, between, True)
    stats_second(1, 1)
    for h in range(2):
        stats_last(1, h)
        weigh_own(1, h)
    for h in range(2):
        share(1, h).wait_recv()
    update(1)

    @pl.loop(0, 56)
    def _(k):
        ref = land.at[pl.ds(0, PIECE)]
        remote(ref, ref, gsend.at[k], grecv.at[0], twin).wait_send()

    for half in range(2):
        ref = land.at[pl.ds(0, 128)]
        remote(ref, ref, gsend.at[56 + half], grecv.at[0], twin).wait_send()

    for it in range(ITERS):
        for h in range(2):
            ref = z1.at[0, 0, 0]
            for k in range(7):
                remote(ref, ref, s1s.at[(it * 2 + h) * 8 + k], s1r.at[0], twin).wait_send()
                remote(ref, ref, s2s.at[(it * 2 + h) * 8 + k], s2r.at[0], twin).wait_send()
            share(it, h).wait_send()

    for h in range(2):
        value = (tot[1, h * 8 : h * 8 + 4, :] + jnp.log2(tot[1, h * 8 + 4 : h * 8 + 8, :])) * LN2
        for j in range(4):
            at = 8 * h + 2 * j
            out_l[at : at + 1, :] = value[j : j + 1, :128]
            out_l[at + 1 : at + 2, :] = value[j : j + 1, 128:]


def local(embeddings, centroids):
    f32, bf16, dma = jnp.float32, jnp.bfloat16, pltpu.SemaphoreType.DMA
    vmem = pltpu.VMEM
    new, logs = pl.pallas_call(
        kernel,
        out_shape=(vmem((K, D), f32), vmem((16, 128), f32)),
        in_specs=[pl.BlockSpec(memory_space=pl.ANY)] * 2,
        out_specs=(pl.BlockSpec(memory_space=vmem), pl.BlockSpec(memory_space=vmem)),
        scratch_shapes=[
            vmem((2 * R, D), bf16),
            vmem((R, D), f32),
            vmem((768, D), f32),
            vmem((K, D), bf16),
            vmem((K, 128), f32),
            vmem((16, K, UNIT), f32),
            vmem((32, UNIT), f32),
            vmem((2, 2, 8, 8, UNIT), f32),
            vmem((2, 2, 8, 8, UNIT), f32),
            vmem((2, 32, UNIT), f32),
            vmem((2, K, D), f32),
            vmem((2, K, 128), f32),
            vmem((H, D), f32),
            vmem((H, 128), f32),
            vmem((2, BLOCK, 4 * UNIT), bf16),
            vmem((K, 2 * UNIT), f32),
            vmem((K, 2 * UNIT), f32),
            dma, dma,
            dma((64,)), dma((64,)),
            dma((32,)), dma((32,)), dma((32,)), dma((32,)),
            dma((4,)), dma((4,)),
            dma((4,)), dma((4,)), dma((4,)), dma((4,)), dma((8,)), dma((8,)),
            pltpu.SemaphoreType.REGULAR((3,)),
        ],
        compiler_params=pltpu.CompilerParams(
            collective_id=0, has_side_effects=True, vmem_limit_bytes=54 << 20
        ),
    )(embeddings, centroids)
    return new, logs.reshape(R)


def solution(mesh):
    placed = (P("dp", None), P("cent", None))
    return jax.shard_map(
        local, mesh=mesh, in_specs=placed, out_specs=(P("cent", None), P("dp")), check_vma=False
    )
```
